128 devices in a mesh: grp: 4 (over x), smp: 32 (over y, z, core).
Axes of the slice: x: 4, y: 4, z: 4, core: 2. Of those that a mesh axis runs over, the one named last changes fastest.
Arguments:
- currents: bfloat16 [2, 8, 1048576], P(None, None, ('grp', 'smp')), may hold values from -6 to 6
- near_blocks: bfloat16 [2, 32768, 32, 256], P(None, ('grp', 'smp')), may hold values from -0.25 to 0.25
- near_list: int32 [32768, 8], P(('grp', 'smp')), may hold values from 0 to 32767, as said below
- near_count: int32 [32768], P(('grp', 'smp')), may hold values from 1 to 8, as said below
- radiation: bfloat16 [2, 32768, 32, 128], P(None, ('grp', 'smp')), may hold values from -0.75 to 0.75
- interp: bfloat16 [64, 1024], replicated, may hold values from -0.75 to 0.75
- shift_angle: float32 [8, 1024], replicated, may hold values from -3.140625 to 3.140625
- translation: bfloat16 [2, 316, 2048], P(None, None, ('grp', 'smp')), may hold values from -0.0625 to 0.0625
- trans_box: int32 [4096, 12], replicated, may hold values from 0 to 4095
- trans_off: int32 [4096, 12], replicated, may hold values from 0 to 315
Outputs:
- product_field: float32 [2, 8, 1048576], P(None, None, ('grp', 'smp'))
The draws below stay inside these ranges and needn't reach their ends.
Inputs may be any that keep to these rules, and one draw needn't show every extreme that they name: `near_list`: entry 0 of row c is c itself, and every entry of row c lies within 256 clusters of c. Slots 0 to near_count[c] - 1 of row c of near_list are live; the other slots are ignored.
All inputs are finite; a program needn't handle non-finite values.
Results may differ from the reference program's by a relative error of at most 0.0056.
Values may be sent and summed in bfloat16 or wider, within the bound.
A program may use at most 128 MiB of HBM per device.

```python
import jax
import jax.numpy as jnp
from jax import lax

R = 8
U = 32
NBR = 8
K0 = 64
K1 = 1024
OFFS = 316
IL = 12
NC = 256
Q0 = 128
Q1 = 2048
CLUSTERS = 32768
UNKNOWNS = 1048576
NB_ALL = 4096


def draw_near_list(key, part):
    key = jax.random.fold_in(key, 11)
    offsets = jax.random.randint(key, (CLUSTERS, NBR), -NC, NC + 1).astype(jnp.int32)
    offsets = offsets.at[:, 0].set(0)
    owners = jnp.arange(CLUSTERS, dtype=jnp.int32)[:, None]
    return jnp.clip(owners + offsets, 0, CLUSTERS - 1).astype(jnp.int32)


def draw_near_count(key, part):
    key = jax.random.fold_in(key, 23)
    first_key, second_key = jax.random.split(key)
    groups = CLUSTERS // NC
    floors = jax.random.randint(first_key, (groups, 1), 1, NBR + 1).astype(jnp.int32)
    counted = jax.random.randint(second_key, (groups, NC), floors, NBR + 1).astype(jnp.int32)
    counted = counted.reshape(CLUSTERS)
    return counted.at[0].set(NBR).astype(jnp.int32)


def place_ends(result, rng, smallest, high):
    longest = result.shape.index(max(result.shape))
    spots = []
    for shift in (0, 1):
        where = [jax.random.randint(jax.random.fold_in(rng, axis), (), 0, length) for axis, length in enumerate(result.shape)]
        where[longest] = (where[longest] + shift) % result.shape[longest]
        spots.append(tuple(where))
    return result.at[spots[0]].set(smallest).at[spots[1]].set(high)


def steps_of(rng, shape, shards, least, largest):
    loudness, own = 1.0, jax.random.fold_in(rng, 6)
    for axis_at, parts in shards:
        draws = jnp.exp(jax.random.uniform(jax.random.fold_in(own, axis_at), (parts,), jnp.float32, least / len(shards), largest / len(shards)))
        loudness = loudness * jnp.repeat(draws, shape[axis_at] // parts).reshape([-1 if axis == axis_at else 1 for axis in range(len(shape))])
    return loudness


def normal_values(own_key, extent, scale, bound, pieces=(), held_as=jnp.bfloat16):
    result = scale * jax.random.normal(own_key, extent, jnp.float32)
    if pieces:
        result = result * steps_of(own_key, extent, pieces, -0.22, 0.18)
    return jnp.clip(result, -bound, bound).astype(held_as)


def setup_inputs(seed: int = 0) -> dict:
    key_list = jax.random.split(jax.random.key(seed), 11)
    return {
        "currents": normal_values(key_list[0], (2, R, UNKNOWNS), 1.0, 6.0, ((2, 128),)),
        "near_blocks": normal_values(key_list[1], (2, CLUSTERS, U, NBR * U), (2 * NBR * U) ** -0.5, 0.25, ((1, 128),)),
        "near_list": draw_near_list(jax.random.fold_in(key_list[10], 71), 0),
        "near_count": draw_near_count(jax.random.fold_in(key_list[10], 71), 0),
        "radiation": normal_values(key_list[4], (2, CLUSTERS, U, Q0), (2 * U) ** -0.5, 0.75, ((1, 128),)),
        "interp": normal_values(key_list[5], (K0, K1), K0 ** -0.5, 0.75),
        "shift_angle": jnp.clip(jax.random.uniform(key_list[6], (8, K1), jnp.float32, -3.140625, 3.140625), -3.140625, 3.140625),
        "translation": normal_values(key_list[7], (2, OFFS, Q1), 0.0113, 0.0625, ((2, 128),)),
        "trans_box": place_ends(jax.random.randint(key_list[8], (NB_ALL, IL), 0, NB_ALL), jax.random.fold_in(key_list[8], 1), 0, NB_ALL - 1).astype(jnp.int32),
        "trans_off": place_ends(jax.random.randint(key_list[9], (NB_ALL, IL), 0, OFFS), jax.random.fold_in(key_list[9], 1), 0, OFFS - 1).astype(jnp.int32),
    }


def product(pattern, left_side, right_side):
    return jnp.einsum(pattern, left_side.astype(jnp.float32), right_side.astype(jnp.float32))


def complex_terms(pattern, left_side, right_side, conjugate):
    if conjugate:
        real_part = product(pattern, left_side[0], right_side[0]) + product(pattern, left_side[1], right_side[1])
        imag_part = product(pattern, left_side[1], right_side[0]) - product(pattern, left_side[0], right_side[1])
    else:
        real_part = product(pattern, left_side[0], right_side[0]) - product(pattern, left_side[1], right_side[1])
        imag_part = product(pattern, left_side[1], right_side[0]) + product(pattern, left_side[0], right_side[1])
    return jnp.stack([real_part, imag_part])


def aggregate(current_block, radiation_block, interp, shift_angle):
    leaf_pattern = complex_terms("rcu,cuq->rcq", current_block, radiation_block, False).astype(jnp.bfloat16)
    clusters_here = leaf_pattern.shape[2]
    upward = jnp.dot(leaf_pattern.reshape(2, R, clusters_here, 2, K0), interp, preferred_element_type=jnp.float32)
    upward = upward.reshape(2, R, clusters_here // 8, 8, 2, K1)
    cosine = jnp.cos(shift_angle)[:, None, :]
    sine_part = jnp.sin(shift_angle)[:, None, :]
    real_part = upward[0] * cosine - upward[1] * sine_part
    imag_part = upward[0] * sine_part + upward[1] * cosine
    summed = jnp.stack([real_part.sum(axis=2), imag_part.sum(axis=2)])
    return summed.reshape(2, R, clusters_here // 8, 2 * K1).astype(jnp.bfloat16)


def disaggregate(received, radiation_block, interp, shift_angle):
    boxes_here = received.shape[2]
    widened = received.astype(jnp.float32).reshape(2, R, boxes_here, 1, 2, K1)
    cosine = jnp.cos(shift_angle)[:, None, :]
    sine_part = jnp.sin(shift_angle)[:, None, :]
    real_part = widened[0] * cosine + widened[1] * sine_part
    imag_part = widened[1] * cosine - widened[0] * sine_part
    shifted = jnp.stack([real_part, imag_part]).astype(jnp.bfloat16)
    downward = jnp.dot(shifted, interp.T, preferred_element_type=jnp.float32).astype(jnp.bfloat16)
    downward = downward.reshape(2, R, boxes_here * 8, 2 * K0)
    return complex_terms("rcq,cuq->rcu", downward, radiation_block, True)


def reference(currents, near_blocks, near_list, near_count, radiation, interp, shift_angle, translation, trans_box, trans_off):
    current_grid = currents.reshape(2, R, CLUSTERS, U)
    blocks = CLUSTERS // NC
    block_ids = jnp.arange(blocks, dtype=jnp.int32)
    slots = jnp.arange(NBR, dtype=jnp.int32)

    def near_block(block_id):
        first_row = (block_id * NC).astype(jnp.int32)
        listed = lax.dynamic_slice_in_dim(near_list, first_row, NC, 0)
        counted = lax.dynamic_slice_in_dim(near_count, first_row, NC, 0)
        live_mask = (slots[None, :] < counted[:, None]).astype(jnp.bfloat16)
        gathered = current_grid[:, :, listed, :] * live_mask[None, None, :, :, None]
        gathered = gathered.reshape(2, R, NC, NBR * U)
        matrices = lax.dynamic_slice_in_dim(near_blocks, first_row, NC, 1)
        return complex_terms("cum,rcm->rcu", matrices, gathered, False)

    def far_up(block_id):
        first_row = (block_id * NC).astype(jnp.int32)
        current_block = lax.dynamic_slice_in_dim(current_grid, first_row, NC, 2)
        radiation_block = lax.dynamic_slice_in_dim(radiation, first_row, NC, 1)
        return aggregate(current_block, radiation_block, interp, shift_angle)

    box_pattern = lax.map(far_up, block_ids)
    box_pattern = box_pattern.transpose(1, 2, 0, 3, 4).reshape(2, R, NB_ALL, Q1)

    def turn(column, totals):
        partner = box_pattern[:, :, trans_box[:, column], :].astype(jnp.float32)
        operator = translation[:, trans_off[:, column], :].astype(jnp.float32)
        real_part = totals[0] + operator[0][None] * partner[0] - operator[1][None] * partner[1]
        imag_part = totals[1] + operator[0][None] * partner[1] + operator[1][None] * partner[0]
        return jnp.stack([real_part, imag_part])

    translated = lax.fori_loop(0, IL, turn, jnp.zeros((2, R, NB_ALL, Q1), jnp.float32)).astype(jnp.bfloat16)

    def far_down(block_id):
        first_row = (block_id * NC).astype(jnp.int32)
        first_box = (block_id * (NC // 8)).astype(jnp.int32)
        received = lax.dynamic_slice_in_dim(translated, first_box, NC // 8, 2)
        radiation_block = lax.dynamic_slice_in_dim(radiation, first_row, NC, 1)
        return disaggregate(received, radiation_block, interp, shift_angle)

    near_field = lax.map(near_block, block_ids)
    far_field = lax.map(far_down, block_ids)
    total = (near_field + far_field).transpose(1, 2, 0, 3, 4)
    return total.reshape(2, R, UNKNOWNS)
```

```python
import functools
import itertools
import random

import jax
import jax.numpy as jnp
from jax import lax
from jax.experimental import pallas as pl
from jax.experimental.pallas import tpu as pltpu
from jax.sharding import PartitionSpec as P

R = 8
U = 32
NBR = 8
K0 = 64
K1 = 1024
IL = 12
NC = 256
OFFS = 316
OFFS_PAD = 320
BOXES = 32
CHIPS = 64
AXES = ("grp", "smp")
MESH_ID = pl.DeviceIdType.MESH
F32 = jnp.float32
BF16 = jnp.bfloat16
VMEM_SPEC = pl.BlockSpec(memory_space=pltpu.VMEM)
SMEM_SPEC = pl.BlockSpec(memory_space=pltpu.SMEM)


def far_first():
    steps = [s for s in itertools.product(range(4), repeat=3) if s != (0, 0, 0)]
    random.Random(1).shuffle(steps)
    return sorted(steps, key=lambda s: -sum(min(a, 4 - a) for a in s))


STEPS = far_first()


def place():
    x = lax.axis_index("grp")
    smp = lax.axis_index("smp")
    core = lax.rem(smp, 2)
    y = lax.div(smp, 8)
    z = lax.rem(lax.div(smp, 2), 4)
    return x, y, z, core


def dot(left, right):
    return lax.dot_general(left, right, (((1,), (0,)), ((), ())), preferred_element_type=F32)


def dot_t(left, right):
    return lax.dot_general(left, right, (((1,), (1,)), ((), ())), preferred_element_type=F32)


def lane_ids(shape):
    return lax.broadcasted_iota(jnp.int32, shape, 1)


def build_matrix(interp, angle, matrix, trig):
    trig[0:8, :] = jnp.cos(angle[...])
    trig[8:16, :] = jnp.sin(angle[...])
    for block in range(8):
        lanes = slice(block * 128, block * 128 + 128)
        table = interp[:, lanes].astype(F32)
        for i in range(8):
            cosine = (table * trig[i : i + 1, lanes]).astype(BF16)
            sine_part = (table * trig[8 + i : 9 + i, lanes]).astype(BF16)
            first = slice(i * 64, i * 64 + 64)
            second = slice(512 + i * 64, 512 + i * 64 + 64)
            matrix[first, block * 256 : block * 256 + 128] = cosine
            matrix[first, block * 256 + 128 : block * 256 + 256] = sine_part
            matrix[second, block * 256 : block * 256 + 128] = -sine_part
            matrix[second, block * 256 + 128 : block * 256 + 256] = cosine


def up_kernel(cur, rad, interp, angle, send, matrix, trig, leaf, packed):
    build_matrix(interp, angle, matrix, trig)
    own = lax.broadcasted_iota(jnp.int32, (128, 256), 0) // 16 == lane_ids((128, 256)) // U
    own = own.astype(F32).astype(BF16)

    def box(b, carry):
        tile = cur[:, pl.ds(pl.multiple_of(b * 256, 256), 256)]
        spread = jnp.concatenate([tile] * 8, axis=0) * own
        real = rad[0, pl.ds(b * 8, 8)].reshape(256, 128)
        imag = rad[1, pl.ds(b * 8, 8)].reshape(256, 128)
        by_real = dot(spread, real)
        by_imag = dot(spread, imag)
        for i in range(8):
            lo = slice(i * 16, i * 16 + 8)
            hi = slice(i * 16 + 8, i * 16 + 16)
            leaf[pl.ds(i * 256 + b, 8, stride=32), :] = by_real[lo] - by_imag[hi]
            leaf[pl.ds((8 + i) * 256 + b, 8, stride=32), :] = by_imag[lo] + by_real[hi]
        return carry

    lax.fori_loop(0, BOXES, box, 0, unroll=2)
    left = lane_ids((256, 128)) < 64
    for c in range(2):
        for m in range(4):
            first = leaf[(c * 8 + 2 * m) * 256 : (c * 8 + 2 * m + 1) * 256, :]
            second = leaf[(c * 8 + 2 * m + 1) * 256 : (c * 8 + 2 * m + 2) * 256, :]
            lanes = slice((c * 4 + m) * 128, (c * 4 + m + 1) * 128)
            packed[0, :, lanes] = jnp.where(left, first, pltpu.roll(second, 64, 1)).astype(BF16)
            packed[1, :, lanes] = jnp.where(left, pltpu.roll(first, 64, 1), second).astype(BF16)
    for p in range(2):
        for block in range(8):
            out = dot(packed[p], matrix[:, block * 256 : block * 256 + 256]).astype(BF16)
            for r in range(R):
                rows = slice(r * 32, r * 32 + 32)
                for c in range(2):
                    send[(p * 8 + block) * 8 + r, c] = out[rows, c * 128 : c * 128 + 128]


def upward(cur, rad, interp, angle):
    return pl.pallas_call(
        up_kernel,
        out_shape=jax.ShapeDtypeStruct((128, 2, BOXES, 128), BF16),
        in_specs=[VMEM_SPEC] * 4,
        out_specs=VMEM_SPEC,
        scratch_shapes=[
            pltpu.VMEM((1024, 2048), BF16),
            pltpu.VMEM((16, 1024), F32),
            pltpu.VMEM((16 * 256, 128), F32),
            pltpu.VMEM((2, 256, 1024), BF16),
        ],
        compiler_params=pltpu.CompilerParams(vmem_limit_bytes=40 << 20),
        name="upward",
    )(cur, rad, interp, angle)


def exchange_kernel(forward, send, rec, send_sems, recv_sems, pass_sems, take_sems, own_sem):
    x, y, z, core = place()
    chip = x * 16 + y * 4 + z
    sibling = (x, (y * 4 + z) * 2 + 1 - core)

    def target(step, sign):
        tx, ty, tz = [lax.rem(a + (4 + sign * s) % 4, 4) for a, s in zip((x, y, z), step)]
        return tx * 16 + ty * 4 + tz, (tx, (ty * 4 + tz) * 2 + core)

    def slot(at):
        return rec.at[2 * at + core] if forward else rec.at[at]

    barrier = pltpu.get_barrier_semaphore()
    for step in STEPS:
        pl.semaphore_signal(barrier, inc=1, device_id=target(step, 1)[1], device_id_type=MESH_ID)
    if forward:
        pl.semaphore_signal(barrier, inc=1, device_id=sibling, device_id_type=MESH_ID)
    pl.semaphore_wait(barrier, len(STEPS) + int(forward))
    copies = []
    for n, step in enumerate(STEPS):
        to, device = target(step, 1)
        copies.append(
            pltpu.make_async_remote_copy(
                src_ref=send.at[to],
                dst_ref=slot(chip),
                send_sem=send_sems.at[n],
                recv_sem=recv_sems.at[n],
                device_id=device,
                device_id_type=MESH_ID,
            )
        )
        copies[-1].start()
    own = pltpu.make_async_copy(send.at[chip], slot(chip), own_sem)
    own.start()
    own.wait()
    if not forward:
        for copy in copies:
            copy.wait()
        return

    passes = []
    for n in range(CHIPS):
        if n == 0:
            source = chip
        else:
            copies[n - 1].wait_recv()
            source = target(STEPS[n - 1], -1)[0]
        passes.append(
            pltpu.make_async_remote_copy(
                src_ref=rec.at[2 * source + core],
                dst_ref=rec.at[2 * source + core],
                send_sem=pass_sems.at[n],
                recv_sem=take_sems.at[n],
                device_id=sibling,
                device_id_type=MESH_ID,
            )
        )
        passes[-1].start()
    for n in range(CHIPS):
        if n > 0:
            copies[n - 1].wait_send()
        passes[n].wait_send()
        source = chip if n == 0 else target(STEPS[n - 1], -1)[0]
        other = rec.at[2 * source + 1 - core]
        pltpu.make_async_copy(other, other, take_sems.at[n]).wait()


def exchange(send, forward):
    return pl.pallas_call(
        functools.partial(exchange_kernel, forward),
        out_shape=jax.ShapeDtypeStruct((128 if forward else 64, 2, 2, BOXES, 128), BF16),
        in_specs=[VMEM_SPEC],
        out_specs=VMEM_SPEC,
        scratch_shapes=[pltpu.SemaphoreType.DMA((CHIPS,))] * 4 + [pltpu.SemaphoreType.DMA],
        compiler_params=pltpu.CompilerParams(
            collective_id=1 if forward else 2, has_side_effects=True, vmem_limit_bytes=40 << 20
        ),
        name="exchange_up" if forward else "exchange_down",
    )(send)


def near_kernel(below, cur, above, blocks, where, out, ext):
    step = pl.program_id(0)

    @pl.when(step == 0)
    def _():
        rows = lax.broadcasted_iota(jnp.int32, (128, 512), 0)
        columns = lane_ids((128, 512))
        copier = jnp.logical_and(rows // U == columns // 128, rows % U == columns % U)
        copier = copier.astype(F32).astype(BF16)
        for part, ref in enumerate((below, cur, above)):

            def fill(g, carry, part=part, ref=ref):
                start = pl.multiple_of(g * 2048, 2048)
                piece = ref[:, pl.ds(start, 2048)]
                stacked = jnp.concatenate([piece[:, k * 128 : k * 128 + 128] for k in range(16)], axis=0)
                wide = dot(stacked, copier).astype(BF16)
                for k in range(16):
                    for j in range(4):
                        row = pl.multiple_of((part * NC + g * 64 + k * 4 + j) * 16, 16)
                        ext[pl.ds(row, 16), :] = wide[k * 16 : k * 16 + 16, j * 128 : j * 128 + 128]
                return carry

            lax.fori_loop(0, 4, fill, 0)
        ext[3 * NC * 16 : 3 * NC * 16 + 16, :] = jnp.zeros((16, 128), BF16)

    masks = [(lane_ids((16, 128)) // U == k).astype(F32).astype(BF16) for k in range(4)]
    own = lane_ids((16, 256)) // U
    for b in range(4):
        gathered = []
        for i in range(8):
            halves = []
            for h in range(2):
                total = None
                for k in range(4):
                    row = where[(step * 4 + b) * 64 + i * 8 + h * 4 + k]
                    piece = ext[pl.ds(pl.multiple_of(row, 16), 16), :] * masks[k]
                    total = piece if total is None else total + piece
                halves.append(total)
            gathered.append(jnp.concatenate(halves, axis=1))
        stacked = jnp.concatenate(gathered, axis=0)
        sums = []
        for c in range(2):
            result = dot_t(stacked, blocks[c, b * 8 : b * 8 + 8].reshape(256, 256))
            total = jnp.zeros((16, 256), F32)
            for i in range(8):
                total = jnp.where(own == i, result[i * 16 : i * 16 + 16], total)
            sums.append(total)
        real, imag = sums
        lanes = slice(b * 256, b * 256 + 256)
        out[0:8, lanes] = real[0:8] - imag[8:16]
        out[8:16, lanes] = imag[0:8] + real[8:16]


def near_part(below, cur, above, blocks, where):
    return pl.pallas_call(
        near_kernel,
        grid=(8,),
        out_shape=jax.ShapeDtypeStruct((16, NC * U), F32),
        in_specs=[
            pl.BlockSpec((16, NC * U), lambda i: (0, 0)),
            pl.BlockSpec((16, NC * U), lambda i: (0, 0)),
            pl.BlockSpec((16, NC * U), lambda i: (0, 0)),
            pl.BlockSpec((2, 32, U, NBR * U), lambda i: (0, i, 0, 0)),
            SMEM_SPEC,
        ],
        out_specs=pl.BlockSpec((16, 1024), lambda i: (0, i)),
        scratch_shapes=[pltpu.VMEM((3 * NC * 16 + 16, 128), BF16)],
        compiler_params=pltpu.CompilerParams(vmem_limit_bytes=40 << 20),
        cost_estimate=pl.CostEstimate(flops=600_000_000, bytes_accessed=9_000_000, transcendentals=0),
        name="near",
    )(below, cur, above, blocks, where)


def translate_kernel(rec, oper, which_box, which_off, out, field, table, sums):
    for k in range(8):
        table[pl.ds(k, OFFS_PAD, stride=8), :] = oper[k // 4]

    def widen(device, carry):
        for k in range(4):
            value = rec[device, k // 2, k % 2].astype(F32)
            field[pl.ds(device * 256 + k, 32, stride=8), :] = value
            field[pl.ds(device * 256 + k + 4, 32, stride=8), :] = value
        return carry

    lax.fori_loop(0, 128, widen, 0)

    def chunk(chip, carry):
        base = chip * (BOXES * IL)
        for b in range(BOXES):
            total = None
            for j in range(IL):
                row = pl.multiple_of(which_box[base + b * IL + j], 8)
                operator = pl.multiple_of(which_off[base + b * IL + j], 8)
                term = field[pl.ds(row, 8), :] * table[pl.ds(operator, 8), :]
                total = term if total is None else total + term
            sums[b * 8 : b * 8 + 8, :] = total
        parts = [sums[pl.ds(k, BOXES, stride=8), :] for k in range(8)]
        out[chip, 0, 0] = (parts[0] - parts[5]).astype(BF16)
        out[chip, 0, 1] = (parts[1] + parts[4]).astype(BF16)
        out[chip, 1, 0] = (parts[2] - parts[7]).astype(BF16)
        out[chip, 1, 1] = (parts[3] + parts[6]).astype(BF16)
        return carry

    lax.fori_loop(0, CHIPS, chunk, 0)


def translate(rec, oper, which_box, which_off):
    return pl.pallas_call(
        translate_kernel,
        out_shape=jax.ShapeDtypeStruct((CHIPS, 2, 2, BOXES, 128), BF16),
        in_specs=[VMEM_SPEC, VMEM_SPEC, SMEM_SPEC, SMEM_SPEC],
        out_specs=VMEM_SPEC,
        scratch_shapes=[
            pltpu.VMEM((4096 * 8, 128), F32),
            pltpu.VMEM((OFFS_PAD * 8, 128), F32),
            pltpu.VMEM((BOXES * 8, 128), F32),
        ],
        compiler_params=pltpu.CompilerParams(vmem_limit_bytes=40 << 20),
        name="translate",
    )(rec, oper, which_box, which_off)


def down_kernel(rec, rad, interp, angle, near, out, matrix, trig, leaf):
    build_matrix(interp, angle, matrix, trig)
    left = lane_ids((256, 128)) < 64
    for c in range(2):
        for half in range(2):
            rows = slice(c * 512 + half * 256, c * 512 + half * 256 + 256)
            results = []
            for p in range(2):
                pieces = []
                for block in range(8):
                    for c2 in range(2):
                        at = (p * 8 + block) * 8
                        pieces.append(rec[at : at + 8, c2].reshape(256, 128))
                fields = jnp.concatenate(pieces, axis=1)
                results.append(dot_t(fields, matrix[rows, :]))
            for m in range(2):
                first = results[0][:, m * 128 : m * 128 + 128]
                second = results[1][:, m * 128 : m * 128 + 128]
                at = (c * 8 + half * 4 + m * 2) * 256
                leaf[at : at + 256, :] = jnp.where(left, first, pltpu.roll(second, 64, 1))
                leaf[at + 256 : at + 512, :] = jnp.where(left, pltpu.roll(first, 64, 1), second)
    own = lane_ids((16, 256)) // U

    def box(b, carry):
        pieces = []
        for i in range(8):
            for c in range(2):
                pieces.append(leaf[pl.ds((c * 8 + i) * 256 + b, 8, stride=32), :])
        stacked = jnp.concatenate(pieces, axis=0).astype(BF16)
        sums = []
        for c in range(2):
            result = dot_t(stacked, rad[c, pl.ds(b * 8, 8)].reshape(256, 128))
            total = jnp.zeros((16, 256), F32)
            for i in range(8):
                total = jnp.where(own == i, result[i * 16 : i * 16 + 16], total)
            sums.append(total)
        real, imag = sums
        lanes = pl.ds(pl.multiple_of(b * 256, 256), 256)
        out[0:8, lanes] = near[0:8, lanes] + (real[0:8] + imag[8:16])
        out[8:16, lanes] = near[8:16, lanes] + (real[8:16] - imag[0:8])
        return carry

    lax.fori_loop(0, BOXES, box, 0, unroll=2)


def downward(rec, rad, interp, angle, near):
    return pl.pallas_call(
        down_kernel,
        out_shape=jax.ShapeDtypeStruct((16, NC * U), F32),
        in_specs=[VMEM_SPEC] * 5,
        out_specs=VMEM_SPEC,
        scratch_shapes=[
            pltpu.VMEM((1024, 2048), BF16),
            pltpu.VMEM((16, 1024), F32),
            pltpu.VMEM((16 * 256, 128), F32),
        ],
        compiler_params=pltpu.CompilerParams(vmem_limit_bytes=40 << 20),
        name="downward",
    )(rec, rad, interp, angle, near)


def passed_along(array, by):
    size = lax.axis_size(AXES)
    pairs = [(i, i + by) for i in range(size) if 0 <= i + by < size]
    return lax.ppermute(array, AXES, pairs)


def local(
    currents,
    near_blocks,
    near_list,
    near_count,
    radiation,
    interp,
    shift_angle,
    translation,
    trans_box,
    trans_off,
):
    device = lax.axis_index(AXES)
    core = lax.rem(device, 2)
    cur = currents.reshape(16, NC * U)
    below = passed_along(cur, 1)
    above = passed_along(cur, -1)
    groups = [list(range(8 * g, 8 * g + 8)) for g in range(4)]
    oper = lax.all_gather(translation, "smp", axis_index_groups=groups, axis=2, tiled=True)
    oper = jnp.pad(oper.astype(F32), ((0, 0), (0, OFFS_PAD - OFFS), (0, 0)))

    slots = jnp.arange(NBR, dtype=jnp.int32)
    row = near_list - (device * NC - NC)
    where = jnp.where(slots[None, :] < near_count[:, None], row, 3 * NC)
    where = (where * 16).reshape(NC * NBR)
    which_box = lax.dynamic_index_in_dim(trans_box.reshape(CHIPS, 2, BOXES * IL), core, 1, False)
    which_off = lax.dynamic_index_in_dim(trans_off.reshape(CHIPS, 2, BOXES * IL), core, 1, False)
    which_box = (which_box * 8).reshape(CHIPS * BOXES * IL)
    which_off = (which_off * 8).reshape(CHIPS * BOXES * IL)

    sent = upward(cur, radiation, interp, shift_angle)
    spread = exchange(sent.reshape(CHIPS, 2, 2, BOXES, 128), True)
    near = near_part(below, cur, above, near_blocks, where)
    translated = translate(spread, oper, which_box, which_off)
    received = exchange(translated, False)
    out = downward(received.reshape(128, 2, BOXES, 128), radiation, interp, shift_angle, near)
    return out.reshape(2, R, NC * U)


def solution(mesh):
    placed = (
        P(None, None, AXES),
        P(None, AXES, None, None),
        P(AXES, None),
        P(AXES),
        P(None, AXES, None, None),
        P(),
        P(),
        P(None, None, AXES),
        P(),
        P(),
    )
    return jax.shard_map(
        local, mesh=mesh, in_specs=placed, out_specs=P(None, None, AXES), check_vma=False
    )
```

```python
import jax
import jax.numpy as jnp
from jax import lax
from jax.experimental import pallas as pl
from jax.experimental.pallas import tpu as pltpu
from jax.sharding import PartitionSpec as P

R = 8
U = 32
NBR = 8
K0 = 64
K1 = 1024
IL = 12
NC = 256
OFFS = 316
BOXES = 32
CHIPS = 64
AXES = ("grp", "smp")
MESH_ID = pl.DeviceIdType.MESH
F32 = jnp.float32
BF16 = jnp.bfloat16
VMEM_SPEC = pl.BlockSpec(memory_space=pltpu.VMEM)
SMEM_SPEC = pl.BlockSpec(memory_space=pltpu.SMEM)


def place():
    x = lax.axis_index("grp")
    smp = lax.axis_index("smp")
    core = lax.rem(smp, 2)
    y = lax.div(smp, 8)
    z = lax.rem(lax.div(smp, 2), 4)
    return x, y, z, core


def dot(left, right):
    return lax.dot_general(left, right, (((1,), (0,)), ((), ())), preferred_element_type=F32)


def dot_t(left, right):
    return lax.dot_general(left, right, (((1,), (1,)), ((), ())), preferred_element_type=F32)


def lane_ids(shape):
    return lax.broadcasted_iota(jnp.int32, shape, 1)


def build_matrix(interp, trig, matrix):
    for block in range(8):
        lanes = slice(block * 128, block * 128 + 128)
        table = interp[:, lanes].astype(F32)
        for i in range(8):
            cosine = (table * trig[i : i + 1, lanes]).astype(BF16)
            sine_part = (table * trig[8 + i : 9 + i, lanes]).astype(BF16)
            first = slice(i * 64, i * 64 + 64)
            second = slice(512 + i * 64, 512 + i * 64 + 64)
            matrix[first, block * 256 : block * 256 + 128] = cosine
            matrix[first, block * 256 + 128 : block * 256 + 256] = sine_part
            matrix[second, block * 256 : block * 256 + 128] = -sine_part
            matrix[second, block * 256 + 128 : block * 256 + 256] = cosine


def leaf_patterns(cur, rad, leaf):
    own = lax.broadcasted_iota(jnp.int32, (128, 256), 0) // 16 == lane_ids((128, 256)) // U
    own = own.astype(F32).astype(BF16)

    def box(b, carry):
        tile = cur[:, pl.ds(pl.multiple_of(b * 256, 256), 256)]
        spread = jnp.concatenate([tile] * 8, axis=0) * own
        real = rad[0, pl.ds(b * 8, 8)].reshape(256, 128)
        imag = rad[1, pl.ds(b * 8, 8)].reshape(256, 128)
        by_real = dot(spread, real)
        by_imag = dot(spread, imag)
        for i in range(8):
            lo = slice(i * 16, i * 16 + 8)
            hi = slice(i * 16 + 8, i * 16 + 16)
            leaf[pl.ds(i * 256 + b, 8, stride=32), :] = by_real[lo] - by_imag[hi]
            leaf[pl.ds((8 + i) * 256 + b, 8, stride=32), :] = by_imag[lo] + by_real[hi]
        return carry

    lax.fori_loop(0, BOXES, box, 0, unroll=2)


def pack_leaves(leaf, packed):
    left = lane_ids((256, 128)) < 64
    for c in range(2):
        for m in range(4):
            first = leaf[(c * 8 + 2 * m) * 256 : (c * 8 + 2 * m + 1) * 256, :]
            second = leaf[(c * 8 + 2 * m + 1) * 256 : (c * 8 + 2 * m + 2) * 256, :]
            lanes = slice((c * 4 + m) * 128, (c * 4 + m + 1) * 128)
            packed[0, :, lanes] = jnp.where(left, first, pltpu.roll(second, 64, 1)).astype(BF16)
            packed[1, :, lanes] = jnp.where(left, pltpu.roll(first, 64, 1), second).astype(BF16)


def spread_currents(window, part, ext):
    rows = lax.broadcasted_iota(jnp.int32, (128, 512), 0)
    columns = lane_ids((128, 512))
    copier = jnp.logical_and(rows // U == columns // 128, rows % U == columns % U)
    copier = copier.astype(F32).astype(BF16)

    def fill(g, carry):
        piece = window[part, :, pl.ds(pl.multiple_of(g * 2048, 2048), 2048)]
        stacked = jnp.concatenate([piece[:, k * 128 : k * 128 + 128] for k in range(16)], axis=0)
        wide = dot(stacked, copier).astype(BF16)
        for k in range(16):
            for j in range(4):
                row = part * NC + g * 64 + k * 4 + j
                ext[row] = wide[k * 16 : k * 16 + 16, j * 128 : j * 128 + 128]
        return carry

    lax.fori_loop(0, 4, fill, 0)


def near_box(b, blocks, where, ext, out):
    masks = [(lane_ids((16, 128)) // U == k).astype(F32).astype(BF16) for k in range(4)]
    own = lane_ids((16, 256)) // U
    gathered = []
    for i in range(8):
        halves = []
        for h in range(2):
            total = None
            for k in range(4):
                row = where[(h * 4 + k) * NC + b * 8 + i]
                piece = ext[row] * masks[k]
                total = piece if total is None else total + piece
            halves.append(total)
        gathered.append(jnp.concatenate(halves, axis=1))
    stacked = jnp.concatenate(gathered, axis=0)
    sums = []
    for c in range(2):
        result = dot_t(stacked, blocks[c, pl.ds(b * 8, 8)].reshape(256, 256))
        total = jnp.zeros((16, 256), F32)
        for i in range(8):
            total = jnp.where(own == i, result[i * 16 : i * 16 + 16], total)
        sums.append(total)
    real, imag = sums
    lanes = pl.ds(pl.multiple_of(b * 256, 256), 256)
    out[0:8, lanes] = real[0:8] - imag[8:16]
    out[8:16, lanes] = imag[0:8] + real[8:16]


def widen(rec, device, field):
    for k in range(4):
        value = rec[device, k // 2, k % 2].astype(F32)
        field[pl.ds(device * 256 + k, 32, stride=8), :] = value
        field[pl.ds(device * 256 + k + 4, 32, stride=8), :] = value


def translate_chunk(base, which_box, which_off, field, table, sums, out, chip):
    for b in range(BOXES):
        total = None
        for j in range(IL):
            row = which_box[base + (j * 4096 + b)]
            operator = which_off[base + (j * 4096 + b)]
            term = field[pl.ds(row, 8), :] * table[pl.ds(operator, 8), :]
            total = term if total is None else total + term
        sums[b * 8 : b * 8 + 8, :] = total
    parts = [sums[pl.ds(k, BOXES, stride=8), :] for k in range(8)]
    out[chip, 0, 0] = (parts[0] - parts[5]).astype(BF16)
    out[chip, 0, 1] = (parts[1] + parts[4]).astype(BF16)
    out[chip, 1, 0] = (parts[2] - parts[7]).astype(BF16)
    out[chip, 1, 1] = (parts[3] + parts[6]).astype(BF16)


def main_kernel(
    cur,
    blocks_in,
    rad_in,
    interp,
    trig,
    oper,
    where,
    box_in,
    off_in,
    rec2,
    near,
    matrix,
    leaf,
    packed,
    rad,
    blocks,
    window,
    ext,
    send,
    rec,
    piece,
    pieces,
    field,
    table,
    sums,
    send2,
    which_box,
    which_off,
    load_sems,
    up_send,
    up_recv,
    pass_send,
    pass_recv,
    down_send,
    down_recv,
    side_send,
    side_recv,
    own_sem,
):
    x, y, z, core = place()
    chip = x * 16 + y * 4 + z
    sibling = (x, (y * 4 + z) * 2 + 1 - core)
    device = chip * 2 + core
    other_at = lax.rem(device + 2 * core - 1 + 128, 128)
    other = (lax.div(other_at, 32), lax.rem(other_at, 32))

    def moved(step, sign):
        tx, ty, tz = [lax.rem(v + 4 + sign * s, 4) for v, s in zip((x, y, z), step)]
        return tx * 16 + ty * 4 + tz, (tx, (ty * 4 + tz) * 2 + core)

    def parted(m):
        return lax.div(m, 16), lax.rem(lax.div(m, 4), 4), lax.rem(m, 4)

    def plane_step(n):
        return lax.rem((n + 1) * 5, 16)

    def up_step(n):
        return parted(plane_step(lax.div(n, 4)) * 4 + lax.rem(lax.rem(n, 4) + 1, 4))

    def down_step(n):
        return parted(lax.rem((n + 1) * 37, CHIPS))

    barrier = pltpu.get_barrier_semaphore()

    def greet(n, carry):
        pl.semaphore_signal(barrier, inc=1, device_id=moved(up_step(n), 1)[1], device_id_type=MESH_ID)
        return carry

    lax.fori_loop(0, CHIPS - 1, greet, 0)
    pl.semaphore_signal(barrier, inc=1, device_id=sibling, device_id_type=MESH_ID)
    pl.semaphore_signal(barrier, inc=1, device_id=other, device_id_type=MESH_ID)

    loads = [
        pltpu.make_async_copy(cur, window.at[1], load_sems.at[0]),
        pltpu.make_async_copy(rad_in, rad, load_sems.at[1]),
        pltpu.make_async_copy(blocks_in, blocks, load_sems.at[2]),
        pltpu.make_async_copy(box_in, which_box, load_sems.at[3]),
        pltpu.make_async_copy(off_in, which_off, load_sems.at[4]),
    ]
    for load in loads:
        load.start()

    build_matrix(interp, trig, matrix)
    piece[...] = jnp.zeros((32, 384), BF16)
    unit = lax.broadcasted_iota(jnp.int32, (16, 16), 0) == lane_ids((16, 16))
    unit = unit.astype(F32).astype(BF16)
    for c in range(2):
        piece[c * 16 : c * 16 + 16, 0:OFFS] = dot_t(unit, oper[c]).astype(BF16)
    loads[0].wait()
    loads[1].wait()
    leaf_patterns(window.at[1], rad, leaf)
    pack_leaves(leaf, packed)

    pl.semaphore_wait(barrier, CHIPS + 1)

    def remote(src, dst, n, to):
        return pltpu.make_async_remote_copy(
            src_ref=src,
            dst_ref=dst,
            send_sem=side_send.at[n],
            recv_sem=side_recv.at[n],
            device_id=to,
            device_id_type=MESH_ID,
        )

    to_sibling = remote(window.at[1], window.at[2 * core], 0, sibling)
    to_other = remote(window.at[1], window.at[2 - 2 * core], 1, other)
    to_sibling.start()
    to_other.start()
    lines = []
    for s in range(3):
        tz = lax.rem(z + s + 1, 4)
        lines.append(remote(piece, pieces.at[z * 2 + core], 2 + s, (x, (y * 4 + tz) * 2 + core)))
        lines[-1].start()
    own_piece = pltpu.make_async_copy(piece, pieces.at[z * 2 + core], load_sems.at[5])
    own_piece.start()

    def up_copy(n):
        to, to_device = moved(up_step(n), 1)
        return pltpu.make_async_remote_copy(
            src_ref=send.at[to],
            dst_ref=rec.at[2 * chip + core],
            send_sem=up_send.at[n],
            recv_sem=up_recv.at[n],
            device_id=to_device,
            device_id_type=MESH_ID,
        )

    def up_block(n, carry):
        plane = plane_step(n)
        kx = lax.rem(x + lax.div(plane, 4), 4)
        ky = lax.rem(y + lax.rem(plane, 4), 4)
        at = kx * 4 + ky
        block = lax.rem(at, 8)
        lanes = pl.ds(pl.multiple_of(block * 256, 256), 256)
        out = dot(packed[lax.div(at, 8)], matrix[:, lanes]).astype(BF16)
        for r in range(R):
            for c in range(2):
                send[at * 4 + r // 2, r % 2, c] = out[r * 32 : r * 32 + 32, c * 128 : c * 128 + 128]
        for s in range(3):
            up_copy(n * 4 + s).start()

        @pl.when(n < 15)
        def _():
            up_copy(n * 4 + 3).start()

        return carry

    lax.fori_loop(0, 16, up_block, 0)
    own = pltpu.make_async_copy(send.at[chip], rec.at[2 * chip + core], own_sem)
    own.start()

    own_piece.wait()
    spread_currents(window, 1, ext)
    ext[3 * NC] = jnp.zeros((16, 128), BF16)
    to_sibling.wait()
    to_other.wait()
    spread_currents(window, 0, ext)
    spread_currents(window, 2, ext)
    loads[2].wait()

    def near_step(b, carry):
        near_box(b, blocks, where, ext, near)
        return carry

    lax.fori_loop(0, BOXES, near_step, 0, unroll=2)

    for line in lines:
        line.wait()
    shares = []
    for s in range(4):
        at = pieces.at[s * 2 + core]
        shares.append(remote(at, at, 5 + s, sibling))
        shares[-1].start()
    own.wait()

    def pass_copy(n, source):
        at = rec.at[2 * source + core]
        return pltpu.make_async_remote_copy(
            src_ref=at,
            dst_ref=at,
            send_sem=pass_send.at[n],
            recv_sem=pass_recv.at[n],
            device_id=sibling,
            device_id_type=MESH_ID,
        )

    pass_copy(CHIPS - 1, chip).start()
    widen(rec, 2 * chip + core, field)

    def arrive(n, carry):
        source = moved(up_step(n), -1)[0]
        up_copy(n).wait_recv()
        pass_copy(n, source).start()
        widen(rec, 2 * source + core, field)
        return carry

    lax.fori_loop(0, CHIPS - 1, arrive, 0)
    for share in shares:
        share.wait()
    for c in range(2):
        rows = [pieces[m, c * 16 : c * 16 + 16, :] for m in range(8)]
        square = jnp.concatenate(rows, axis=0).astype(F32)
        for g in range(3):
            turned = square[:, g * 128 : g * 128 + 128].T
            for k in range(4):
                table[pl.ds(g * 1024 + c * 4 + k, 128, stride=8), :] = turned

    def take(n, carry):
        source = moved(up_step(n), -1)[0]
        at = rec.at[2 * source + 1 - core]
        pltpu.make_async_copy(at, at, pass_recv.at[n]).wait()
        widen(rec, 2 * source + 1 - core, field)
        return carry

    lax.fori_loop(0, CHIPS, take, 0)

    def up_done(n, carry):
        up_copy(n).wait_send()
        pass_copy(n, moved(up_step(n), -1)[0]).wait_send()
        return carry

    lax.fori_loop(0, CHIPS - 1, up_done, 0)
    pass_copy(CHIPS - 1, chip).wait_send()
    loads[3].wait()
    loads[4].wait()

    def down_copy(n):
        to, to_device = moved(down_step(n), 1)
        return pltpu.make_async_remote_copy(
            src_ref=send2.at[to],
            dst_ref=rec2.at[chip],
            send_sem=down_send.at[n],
            recv_sem=down_recv.at[n],
            device_id=to_device,
            device_id_type=MESH_ID,
        )

    def chunk(n, carry):
        to = moved(down_step(n), 1)[0]
        base = to * 64 + core * 32
        translate_chunk(base, which_box, which_off, field, table, sums, send2, to)

        @pl.when(n < CHIPS - 1)
        def _():
            down_copy(n).start()

        return carry

    lax.fori_loop(0, CHIPS, chunk, 0)
    last = pltpu.make_async_copy(send2.at[chip], rec2.at[chip], own_sem)
    last.start()
    last.wait()

    def down_done(n, carry):
        down_copy(n).wait()
        return carry

    lax.fori_loop(0, CHIPS - 1, down_done, 0)


def main_part(cur, blocks, rad, interp, trig, oper, where, which_box, which_off):
    any_spec = pl.BlockSpec(memory_space=pl.ANY)
    sems = pltpu.SemaphoreType.DMA
    return pl.pallas_call(
        main_kernel,
        out_shape=(
            jax.ShapeDtypeStruct((CHIPS, 2, 2, BOXES, 128), BF16),
            jax.ShapeDtypeStruct((16, NC * U), F32),
        ),
        in_specs=[any_spec] * 3 + [VMEM_SPEC] * 3 + [SMEM_SPEC] + [any_spec] * 2,
        out_specs=(VMEM_SPEC, VMEM_SPEC),
        scratch_shapes=[
            pltpu.VMEM((1024, 2048), BF16),
            pltpu.VMEM((16 * 256, 128), F32),
            pltpu.VMEM((2, 256, 1024), BF16),
            pltpu.VMEM((2, NC, U, 128), BF16),
            pltpu.VMEM((2, NC, U, NBR * U), BF16),
            pltpu.VMEM((3, 16, NC * U), BF16),
            pltpu.VMEM((3 * NC + 1, 16, 128), BF16),
            pltpu.VMEM((CHIPS, 2, 2, BOXES, 128), BF16),
            pltpu.VMEM((2 * CHIPS, 2, 2, BOXES, 128), BF16),
            pltpu.VMEM((32, 384), BF16),
            pltpu.VMEM((8, 32, 384), BF16),
            pltpu.VMEM((4096 * 8, 128), F32),
            pltpu.VMEM((384 * 8, 128), F32),
            pltpu.VMEM((BOXES * 8, 128), F32),
            pltpu.VMEM((CHIPS, 2, 2, BOXES, 128), BF16),
            pltpu.SMEM((4096 * IL,), jnp.int32),
            pltpu.SMEM((4096 * IL,), jnp.int32),
            sems((6,)),
            sems((CHIPS,)),
            sems((CHIPS,)),
            sems((CHIPS,)),
            sems((CHIPS,)),
            sems((CHIPS,)),
            sems((CHIPS,)),
            sems((9,)),
            sems((9,)),
            sems,
        ],
        compiler_params=pltpu.CompilerParams(
            collective_id=1, has_side_effects=True, vmem_limit_bytes=60 << 20
        ),
        name="up_near_translate",
    )(cur, blocks, rad, interp, trig, oper, where, which_box, which_off)


def down_kernel(rec, rad, interp, trig, near, out, matrix, leaf):
    build_matrix(interp, trig, matrix)
    left = lane_ids((256, 128)) < 64
    for c in range(2):
        for half in range(2):
            rows = slice(c * 512 + half * 256, c * 512 + half * 256 + 256)
            results = []
            for p in range(2):
                pieces = []
                for block in range(8):
                    for c2 in range(2):
                        at = (p * 8 + block) * 8
                        pieces.append(rec[at : at + 8, c2].reshape(256, 128))
                fields = jnp.concatenate(pieces, axis=1)
                results.append(dot_t(fields, matrix[rows, :]))
            for m in range(2):
                first = results[0][:, m * 128 : m * 128 + 128]
                second = results[1][:, m * 128 : m * 128 + 128]
                at = (c * 8 + half * 4 + m * 2) * 256
                leaf[at : at + 256, :] = jnp.where(left, first, pltpu.roll(second, 64, 1))
                leaf[at + 256 : at + 512, :] = jnp.where(left, pltpu.roll(first, 64, 1), second)
    own = lane_ids((16, 256)) // U

    def box(b, carry):
        pieces = []
        for i in range(8):
            for c in range(2):
                pieces.append(leaf[pl.ds((c * 8 + i) * 256 + b, 8, stride=32), :])
        stacked = jnp.concatenate(pieces, axis=0).astype(BF16)
        sums = []
        for c in range(2):
            result = dot_t(stacked, rad[c, pl.ds(b * 8, 8)].reshape(256, 128))
            total = jnp.zeros((16, 256), F32)
            for i in range(8):
                total = jnp.where(own == i, result[i * 16 : i * 16 + 16], total)
            sums.append(total)
        real, imag = sums
        lanes = pl.ds(pl.multiple_of(b * 256, 256), 256)
        out[0:8, lanes] = near[0:8, lanes] + (real[0:8] + imag[8:16])
        out[8:16, lanes] = near[8:16, lanes] + (real[8:16] - imag[0:8])
        return carry

    lax.fori_loop(0, BOXES, box, 0, unroll=2)


def downward(rec, rad, interp, trig, near):
    return pl.pallas_call(
        down_kernel,
        out_shape=jax.ShapeDtypeStruct((16, NC * U), F32),
        in_specs=[VMEM_SPEC] * 5,
        out_specs=VMEM_SPEC,
        scratch_shapes=[
            pltpu.VMEM((1024, 2048), BF16),
            pltpu.VMEM((16 * 256, 128), F32),
        ],
        compiler_params=pltpu.CompilerParams(vmem_limit_bytes=40 << 20),
        name="downward",
    )(rec, rad, interp, trig, near)


def local(
    currents,
    near_blocks,
    near_list,
    near_count,
    radiation,
    interp,
    shift_angle,
    translation,
    trans_box,
    trans_off,
):
    device = lax.axis_index(AXES)
    cur = currents.reshape(16, NC * U)
    slots = jnp.arange(NBR, dtype=jnp.int32)
    row = near_list.T - (device * NC - NC)
    where = jnp.where(slots[:, None] < near_count[None, :], row, 3 * NC)
    where = where.reshape(NC * NBR)
    which_box = (trans_box.T * 8).reshape(4096 * IL)
    which_off = (trans_off.T * 8).reshape(4096 * IL)
    trig = jnp.concatenate([jnp.cos(shift_angle), jnp.sin(shift_angle)], axis=0)
    received, near = main_part(
        cur, near_blocks, radiation, interp, trig, translation, where, which_box, which_off
    )
    out = downward(received.reshape(128, 2, BOXES, 128), radiation, interp, trig, near)
    return out.reshape(2, R, NC * U)


def solution(mesh):
    placed = (
        P(None, None, AXES),
        P(None, AXES, None, None),
        P(AXES, None),
        P(AXES),
        P(None, AXES, None, None),
        P(),
        P(),
        P(None, None, AXES),
        P(),
        P(),
    )
    return jax.shard_map(
        local, mesh=mesh, in_specs=placed, out_specs=P(None, None, AXES), check_vma=False
    )
```

```python
import jax
import jax.numpy as jnp
from jax import lax
from jax.experimental import pallas as pl
from jax.experimental.pallas import tpu as pltpu
from jax.sharding import PartitionSpec as P

R = 8
U = 32
NBR = 8
K0 = 64
K1 = 1024
IL = 12
NC = 256
OFFS = 316
BOXES = 32
CHIPS = 64
AXES = ("grp", "smp")
MESH_ID = pl.DeviceIdType.MESH
F32 = jnp.float32
BF16 = jnp.bfloat16
VMEM_SPEC = pl.BlockSpec(memory_space=pltpu.VMEM)
SMEM_SPEC = pl.BlockSpec(memory_space=pltpu.SMEM)


def place():
    x = lax.axis_index("grp")
    smp = lax.axis_index("smp")
    core = lax.rem(smp, 2)
    y = lax.div(smp, 8)
    z = lax.rem(lax.div(smp, 2), 4)
    return x, y, z, core


def dot(left, right):
    return lax.dot_general(left, right, (((1,), (0,)), ((), ())), preferred_element_type=F32)


def dot_t(left, right):
    return lax.dot_general(left, right, (((1,), (1,)), ((), ())), preferred_element_type=F32)


def lane_ids(shape):
    return lax.broadcasted_iota(jnp.int32, shape, 1)


def build_matrix(interp, angle, matrix, trig):
    trig[0:8, :] = jnp.cos(angle[...])
    trig[8:16, :] = jnp.sin(angle[...])
    for block in range(8):
        lanes = slice(block * 128, block * 128 + 128)
        table = interp[:, lanes].astype(F32)
        for i in range(8):
            cosine = (table * trig[i : i + 1, lanes]).astype(BF16)
            sine_part = (table * trig[8 + i : 9 + i, lanes]).astype(BF16)
            first = slice(i * 64, i * 64 + 64)
            second = slice(512 + i * 64, 512 + i * 64 + 64)
            matrix[first, block * 256 : block * 256 + 128] = cosine
            matrix[first, block * 256 + 128 : block * 256 + 256] = sine_part
            matrix[second, block * 256 : block * 256 + 128] = -sine_part
            matrix[second, block * 256 + 128 : block * 256 + 256] = cosine


def leaf_patterns(cur, rad, leaf):
    own = lax.broadcasted_iota(jnp.int32, (128, 256), 0) // 16 == lane_ids((128, 256)) // U
    own = own.astype(F32).astype(BF16)

    def box(b, carry):
        tile = cur[:, pl.ds(pl.multiple_of(b * 256, 256), 256)]
        spread = jnp.concatenate([tile] * 8, axis=0) * own
        real = rad[0, pl.ds(b * 8, 8)].reshape(256, 128)
        imag = rad[1, pl.ds(b * 8, 8)].reshape(256, 128)
        by_real = dot(spread, real)
        by_imag = dot(spread, imag)
        for i in range(8):
            lo = slice(i * 16, i * 16 + 8)
            hi = slice(i * 16 + 8, i * 16 + 16)
            leaf[pl.ds(i * 256 + b, 8, stride=32), :] = by_real[lo] - by_imag[hi]
            leaf[pl.ds((8 + i) * 256 + b, 8, stride=32), :] = by_imag[lo] + by_real[hi]
        return carry

    lax.fori_loop(0, BOXES, box, 0, unroll=2)


def pack_leaves(leaf, packed):
    left = lane_ids((256, 128)) < 64
    for c in range(2):
        for m in range(4):
            first = leaf[(c * 8 + 2 * m) * 256 : (c * 8 + 2 * m + 1) * 256, :]
            second = leaf[(c * 8 + 2 * m + 1) * 256 : (c * 8 + 2 * m + 2) * 256, :]
            lanes = slice((c * 4 + m) * 128, (c * 4 + m + 1) * 128)
            packed[0, :, lanes] = jnp.where(left, first, pltpu.roll(second, 64, 1)).astype(BF16)
            packed[1, :, lanes] = jnp.where(left, pltpu.roll(first, 64, 1), second).astype(BF16)


def spread_currents(window, part, ext):
    rows = lax.broadcasted_iota(jnp.int32, (128, 512), 0)
    columns = lane_ids((128, 512))
    copier = jnp.logical_and(rows // U == columns // 128, rows % U == columns % U)
    copier = copier.astype(F32).astype(BF16)

    def fill(g, carry):
        piece = window[part, :, pl.ds(pl.multiple_of(g * 2048, 2048), 2048)]
        stacked = jnp.concatenate([piece[:, k * 128 : k * 128 + 128] for k in range(16)], axis=0)
        wide = dot(stacked, copier).astype(BF16)
        for k in range(16):
            for j in range(4):
                row = part * NC + g * 64 + k * 4 + j
                ext[row] = wide[k * 16 : k * 16 + 16, j * 128 : j * 128 + 128]
        return carry

    lax.fori_loop(0, 4, fill, 0)


def near_box(b, blocks, where, ext, out):
    masks = [(lane_ids((16, 128)) // U == k).astype(F32).astype(BF16) for k in range(4)]
    own = lane_ids((16, 256)) // U
    gathered = []
    for i in range(8):
        halves = []
        for h in range(2):
            total = None
            for k in range(4):
                row = where[(h * 4 + k) * NC + b * 8 + i]
                piece = ext[row] * masks[k]
                total = piece if total is None else total + piece
            halves.append(total)
        gathered.append(jnp.concatenate(halves, axis=1))
    stacked = jnp.concatenate(gathered, axis=0)
    sums = []
    for c in range(2):
        result = dot_t(stacked, blocks[c, pl.ds(b * 8, 8)].reshape(256, 256))
        total = jnp.zeros((16, 256), F32)
        for i in range(8):
            total = jnp.where(own == i, result[i * 16 : i * 16 + 16], total)
        sums.append(total)
    real, imag = sums
    lanes = pl.ds(pl.multiple_of(b * 256, 256), 256)
    out[0:8, lanes] = real[0:8] - imag[8:16]
    out[8:16, lanes] = imag[0:8] + real[8:16]


def widen(rec, device, field):
    for k in range(4):
        value = rec[device, k // 2, k % 2].astype(F32)
        field[pl.ds(device * 256 + k, 32, stride=8), :] = value
        field[pl.ds(device * 256 + k + 4, 32, stride=8), :] = value


def translate_chunk(base, which_box, which_off, field, table, sums, out, chip):
    for b in range(BOXES):
        total = None
        for j in range(IL):
            row = which_box[base + (j * 4096 + b)]
            operator = which_off[base + (j * 4096 + b)]
            term = field[pl.ds(row, 8), :] * table[pl.ds(operator, 8), :]
            total = term if total is None else total + term
        sums[b * 8 : b * 8 + 8, :] = total
    parts = [sums[pl.ds(k, BOXES, stride=8), :] for k in range(8)]
    out[chip, 0, 0] = (parts[0] - parts[5]).astype(BF16)
    out[chip, 0, 1] = (parts[1] + parts[4]).astype(BF16)
    out[chip, 1, 0] = (parts[2] - parts[7]).astype(BF16)
    out[chip, 1, 1] = (parts[3] + parts[6]).astype(BF16)


def unpack_fields(rec2, matrix, leaf):
    left = lane_ids((256, 128)) < 64
    for c in range(2):
        for half in range(2):
            rows = slice(c * 512 + half * 256, c * 512 + half * 256 + 256)
            results = []
            for p in range(2):
                pieces = []
                for block in range(8):
                    for c2 in range(2):
                        at = (p * 8 + block) * 4
                        pieces.append(rec2[at : at + 4, :, c2].reshape(256, 128))
                fields = jnp.concatenate(pieces, axis=1)
                results.append(dot_t(fields, matrix[rows, :]))
            for m in range(2):
                first = results[0][:, m * 128 : m * 128 + 128]
                second = results[1][:, m * 128 : m * 128 + 128]
                at = (c * 8 + half * 4 + m * 2) * 256
                leaf[at : at + 256, :] = jnp.where(left, first, pltpu.roll(second, 64, 1))
                leaf[at + 256 : at + 512, :] = jnp.where(left, pltpu.roll(first, 64, 1), second)


def far_boxes(leaf, rad, out):
    own = lane_ids((16, 256)) // U

    def box(b, carry):
        pieces = []
        for i in range(8):
            for c in range(2):
                pieces.append(leaf[pl.ds((c * 8 + i) * 256 + b, 8, stride=32), :])
        stacked = jnp.concatenate(pieces, axis=0).astype(BF16)
        sums = []
        for c in range(2):
            result = dot_t(stacked, rad[c, pl.ds(b * 8, 8)].reshape(256, 128))
            total = jnp.zeros((16, 256), F32)
            for i in range(8):
                total = jnp.where(own == i, result[i * 16 : i * 16 + 16], total)
            sums.append(total)
        real, imag = sums
        lanes = pl.ds(pl.multiple_of(b * 256, 256), 256)
        out[0:8, lanes] += real[0:8] + imag[8:16]
        out[8:16, lanes] += real[8:16] - imag[0:8]
        return carry

    lax.fori_loop(0, BOXES, box, 0, unroll=2)


def main_kernel(
    cur,
    blocks_in,
    rad_in,
    interp,
    angle,
    oper,
    list_in,
    count_in,
    box_in,
    off_in,
    out,
    matrix,
    trig,
    leaf,
    packed,
    rad,
    blocks,
    window,
    ext,
    send,
    rec,
    piece,
    pieces,
    field,
    table,
    sums,
    send2,
    rec2,
    rows_here,
    boxes_here,
    offs_here,
    where,
    which_box,
    which_off,
    load_sems,
    list_sems,
    box_sems,
    off_sems,
    up_send,
    up_recv,
    pass_send,
    pass_recv,
    down_send,
    down_recv,
    side_send,
    side_recv,
    own_sem,
):
    x, y, z, core = place()
    chip = x * 16 + y * 4 + z
    sibling = (x, (y * 4 + z) * 2 + 1 - core)
    device = chip * 2 + core
    other_at = lax.rem(device + 2 * core - 1 + 128, 128)
    other = (lax.div(other_at, 32), lax.rem(other_at, 32))

    def moved(n, sign):
        m = lax.rem((n + 1) * 37, CHIPS)
        step = (lax.div(m, 16), lax.rem(lax.div(m, 4), 4), lax.rem(m, 4))
        tx, ty, tz = [lax.rem(v + 4 + sign * s, 4) for v, s in zip((x, y, z), step)]
        return tx * 16 + ty * 4 + tz, (tx, (ty * 4 + tz) * 2 + core)

    loads = [
        pltpu.make_async_copy(cur, window.at[1], load_sems.at[0]),
        pltpu.make_async_copy(rad_in, rad, load_sems.at[1]),
        pltpu.make_async_copy(blocks_in, blocks, load_sems.at[2]),
    ]
    for load in loads:
        load.start()
    barrier = pltpu.get_barrier_semaphore()

    def greet(n, carry):
        pl.semaphore_signal(barrier, inc=1, device_id=moved(n, 1)[1], device_id_type=MESH_ID)
        return carry

    lax.fori_loop(0, CHIPS - 1, greet, 0)
    pl.semaphore_signal(barrier, inc=1, device_id=sibling, device_id_type=MESH_ID)
    pl.semaphore_signal(barrier, inc=1, device_id=other, device_id_type=MESH_ID)

    slots = lax.broadcasted_iota(jnp.int32, (NBR, NC), 0)
    rows_here[...] = jnp.where(slots < count_in[...], list_in[...] - (device * NC - NC), 3 * NC)
    boxes_here[...] = box_in[...] * 8
    offs_here[...] = off_in[...] * 8
    lists = []
    for k in range(NBR):
        lists.append(
            pltpu.make_async_copy(rows_here.at[k], where.at[pl.ds(k * NC, NC)], list_sems.at[k])
        )
    for j in range(IL):
        part = pl.ds(j * 4096, 4096)
        lists.append(pltpu.make_async_copy(boxes_here.at[j], which_box.at[part], box_sems.at[j]))
        lists.append(pltpu.make_async_copy(offs_here.at[j], which_off.at[part], off_sems.at[j]))
    for copy in lists:
        copy.start()

    build_matrix(interp, angle, matrix, trig)
    piece[...] = jnp.zeros((32, 384), BF16)
    for c in range(2):
        piece[c * 16 : c * 16 + 16, 0:OFFS] = oper[c]
    loads[0].wait()
    loads[1].wait()
    leaf_patterns(window.at[1], rad, leaf)
    pack_leaves(leaf, packed)
    for at in range(16):
        lanes = slice(at % 8 * 256, at % 8 * 256 + 256)
        result = dot(packed[at // 8], matrix[:, lanes]).astype(BF16)
        for r in range(R):
            for c in range(2):
                send[at * 4 + r // 2, r % 2, c] = result[r * 32 : r * 32 + 32, c * 128 : c * 128 + 128]

    pl.semaphore_wait(barrier, CHIPS + 1)

    def remote(src, dst, n, to):
        return pltpu.make_async_remote_copy(
            src_ref=src,
            dst_ref=dst,
            send_sem=side_send.at[n],
            recv_sem=side_recv.at[n],
            device_id=to,
            device_id_type=MESH_ID,
        )

    to_sibling = remote(window.at[1], window.at[2 * core], 0, sibling)
    to_other = remote(window.at[1], window.at[2 - 2 * core], 1, other)
    to_sibling.start()
    to_other.start()
    lines = []
    for s in range(3):
        tz = lax.rem(z + s + 1, 4)
        lines.append(remote(piece, pieces.at[z * 2 + core], 2 + s, (x, (y * 4 + tz) * 2 + core)))
        lines[-1].start()

    def up_copy(n):
        to, to_device = moved(n, 1)
        return pltpu.make_async_remote_copy(
            src_ref=send.at[to],
            dst_ref=rec.at[2 * chip + core],
            send_sem=up_send.at[n],
            recv_sem=up_recv.at[n],
            device_id=to_device,
            device_id_type=MESH_ID,
        )

    def up_start(n, carry):
        up_copy(n).start()
        return carry

    lax.fori_loop(0, CHIPS - 1, up_start, 0)
    own_piece = pltpu.make_async_copy(piece, pieces.at[z * 2 + core], load_sems.at[3])
    own_piece.start()
    own = pltpu.make_async_copy(send.at[chip], rec.at[2 * chip + core], own_sem)
    own.start()

    own_piece.wait()
    for line in lines:
        line.wait()
    shares = []
    for s in range(4):
        at = pieces.at[s * 2 + core]
        shares.append(remote(at, at, 5 + s, sibling))
        shares[-1].start()
    own.wait()

    def pass_copy(n):
        at = rec.at[2 * moved(n, -1)[0] + core]
        return pltpu.make_async_remote_copy(
            src_ref=at,
            dst_ref=at,
            send_sem=pass_send.at[n],
            recv_sem=pass_recv.at[n],
            device_id=sibling,
            device_id_type=MESH_ID,
        )

    pass_copy(CHIPS - 1).start()
    widen(rec, 2 * chip + core, field)
    spread_currents(window, 1, ext)
    ext[3 * NC] = jnp.zeros((16, 128), BF16)
    to_sibling.wait()
    to_other.wait()
    spread_currents(window, 0, ext)
    spread_currents(window, 2, ext)
    for share in shares:
        share.wait()
    for c in range(2):
        rows = [pieces[m, c * 16 : c * 16 + 16, :] for m in range(8)]
        square = jnp.concatenate(rows, axis=0).astype(F32)
        for g in range(3):
            turned = square[:, g * 128 : g * 128 + 128].T
            for k in range(4):
                table[pl.ds(g * 1024 + c * 4 + k, 128, stride=8), :] = turned
    loads[2].wait()
    for copy in lists:
        copy.wait()

    def arrive(n):
        up_copy(n).wait_recv()
        pass_copy(n).start()
        widen(rec, 2 * moved(n, -1)[0] + core, field)

    def take(n):
        source = moved(n, -1)[0]
        at = rec.at[2 * source + 1 - core]
        pltpu.make_async_copy(at, at, pass_recv.at[n]).wait()
        widen(rec, 2 * source + 1 - core, field)

    def near_step(b, carry):
        near_box(b, blocks, where, ext, out)
        arrive(2 * b)

        @pl.when(b < 31)
        def _():
            arrive(2 * b + 1)

        @pl.when(b >= 2)
        def _():
            take(2 * b - 4)
            take(2 * b - 3)

        return carry

    lax.fori_loop(0, BOXES, near_step, 0)
    for n in range(CHIPS - 4, CHIPS):
        take(n)

    def down_copy(n):
        to, to_device = moved(n, 1)
        return pltpu.make_async_remote_copy(
            src_ref=send2.at[to],
            dst_ref=rec2.at[chip],
            send_sem=down_send.at[n],
            recv_sem=down_recv.at[n],
            device_id=to_device,
            device_id_type=MESH_ID,
        )

    def chunk(n, carry):
        to = moved(n, 1)[0]
        base = to * 64 + core * 32
        translate_chunk(base, which_box, which_off, field, table, sums, send2, to)

        @pl.when(n < CHIPS - 1)
        def _():
            down_copy(n).start()

        return carry

    lax.fori_loop(0, CHIPS, chunk, 0)
    last = pltpu.make_async_copy(send2.at[chip], rec2.at[chip], own_sem)
    last.start()

    def up_done(n, carry):
        up_copy(n).wait_send()
        pass_copy(n).wait_send()
        return carry

    lax.fori_loop(0, CHIPS - 1, up_done, 0)
    pass_copy(CHIPS - 1).wait_send()
    last.wait()

    def down_done(n, carry):
        down_copy(n).wait()
        return carry

    lax.fori_loop(0, CHIPS - 1, down_done, 0)
    unpack_fields(rec2, matrix, leaf)
    far_boxes(leaf, rad, out)


def main_part(cur, blocks, rad, interp, angle, oper, near_rows, near_count, box, off):
    any_spec = pl.BlockSpec(memory_space=pl.ANY)
    sems = pltpu.SemaphoreType.DMA
    return pl.pallas_call(
        main_kernel,
        out_shape=jax.ShapeDtypeStruct((16, NC * U), F32),
        in_specs=[any_spec] * 3 + [VMEM_SPEC] * 7,
        out_specs=VMEM_SPEC,
        scratch_shapes=[
            pltpu.VMEM((1024, 2048), BF16),
            pltpu.VMEM((16, 1024), F32),
            pltpu.VMEM((16 * 256, 128), F32),
            pltpu.VMEM((2, 256, 1024), BF16),
            pltpu.VMEM((2, NC, U, 128), BF16),
            pltpu.VMEM((2, NC, U, NBR * U), BF16),
            pltpu.VMEM((3, 16, NC * U), BF16),
            pltpu.VMEM((3 * NC + 1, 16, 128), BF16),
            pltpu.VMEM((CHIPS, 2, 2, BOXES, 128), BF16),
            pltpu.VMEM((2 * CHIPS, 2, 2, BOXES, 128), BF16),
            pltpu.VMEM((32, 384), BF16),
            pltpu.VMEM((8, 32, 384), BF16),
            pltpu.VMEM((4096 * 8, 128), F32),
            pltpu.VMEM((384 * 8, 128), F32),
            pltpu.VMEM((BOXES * 8, 128), F32),
            pltpu.VMEM((CHIPS, 2, 2, BOXES, 128), BF16),
            pltpu.VMEM((CHIPS, 2, 2, BOXES, 128), BF16),
            pltpu.VMEM((NBR, NC), jnp.int32),
            pltpu.VMEM((IL, 4096), jnp.int32),
            pltpu.VMEM((IL, 4096), jnp.int32),
            pltpu.SMEM((NC * NBR,), jnp.int32),
            pltpu.SMEM((4096 * IL,), jnp.int32),
            pltpu.SMEM((4096 * IL,), jnp.int32),
            sems((4,)),
            sems((NBR,)),
            sems((IL,)),
            sems((IL,)),
            sems((CHIPS,)),
            sems((CHIPS,)),
            sems((CHIPS,)),
            sems((CHIPS,)),
            sems((CHIPS,)),
            sems((CHIPS,)),
            sems((9,)),
            sems((9,)),
            sems,
        ],
        compiler_params=pltpu.CompilerParams(
            collective_id=1, has_side_effects=True, vmem_limit_bytes=60 << 20
        ),
        name="up_near_translate",
    )(cur, blocks, rad, interp, angle, oper, near_rows, near_count, box, off)


def local(
    currents,
    near_blocks,
    near_list,
    near_count,
    radiation,
    interp,
    shift_angle,
    translation,
    trans_box,
    trans_off,
):
    out = main_part(
        currents.reshape(16, NC * U),
        near_blocks,
        radiation,
        interp,
        shift_angle,
        translation.transpose(0, 2, 1),
        near_list.T,
        near_count.reshape(1, NC),
        trans_box.T,
        trans_off.T,
    )
    return out.reshape(2, R, NC * U)


def solution(mesh):
    placed = (
        P(None, None, AXES),
        P(None, AXES, None, None),
        P(AXES, None),
        P(AXES),
        P(None, AXES, None, None),
        P(),
        P(),
        P(None, None, AXES),
        P(),
        P(),
    )
    return jax.shard_map(
        local, mesh=mesh, in_specs=placed, out_specs=P(None, None, AXES), check_vma=False
    )
```

```python
import jax
import jax.numpy as jnp
from jax import lax
from jax.experimental import pallas as pl
from jax.experimental.pallas import tpu as pltpu
from jax.sharding import PartitionSpec as P

R = 8
U = 32
NBR = 8
K0 = 64
K1 = 1024
IL = 12
NC = 256
OFFS = 316
BOXES = 32
WINDOW = 32
GROUP = 4
CHIPS = 64
AXES = ("grp", "smp")
MESH_ID = pl.DeviceIdType.MESH
F32 = jnp.float32
BF16 = jnp.bfloat16
VMEM_SPEC = pl.BlockSpec(memory_space=pltpu.VMEM)
SMEM_SPEC = pl.BlockSpec(memory_space=pltpu.SMEM)


def place():
    x = lax.axis_index("grp")
    smp = lax.axis_index("smp")
    core = lax.rem(smp, 2)
    y = lax.div(smp, 8)
    z = lax.rem(lax.div(smp, 2), 4)
    return x, y, z, core


def dot(left, right):
    return lax.dot_general(left, right, (((1,), (0,)), ((), ())), preferred_element_type=F32)


def dot_t(left, right):
    return lax.dot_general(left, right, (((1,), (1,)), ((), ())), preferred_element_type=F32)


def lane_ids(shape):
    return lax.broadcasted_iota(jnp.int32, shape, 1)


def build_matrix(interp, angle, matrix, trig):
    trig[0:8, :] = jnp.cos(angle[...])
    trig[8:16, :] = jnp.sin(angle[...])
    for block in range(8):
        lanes = slice(block * 128, block * 128 + 128)
        table = interp[:, lanes].astype(F32)
        for i in range(8):
            cosine = (table * trig[i : i + 1, lanes]).astype(BF16)
            sine_part = (table * trig[8 + i : 9 + i, lanes]).astype(BF16)
            first = slice(i * 64, i * 64 + 64)
            second = slice(512 + i * 64, 512 + i * 64 + 64)
            matrix[first, block * 256 : block * 256 + 128] = cosine
            matrix[first, block * 256 + 128 : block * 256 + 256] = sine_part
            matrix[second, block * 256 : block * 256 + 128] = -sine_part
            matrix[second, block * 256 + 128 : block * 256 + 256] = cosine


def leaf_patterns(cur, rad, leaf):
    own = lax.broadcasted_iota(jnp.int32, (128, 256), 0) // 16 == lane_ids((128, 256)) // U
    own = own.astype(F32).astype(BF16)

    def box(b, carry):
        tile = cur[:, pl.ds(pl.multiple_of(b * 256, 256), 256)]
        spread = jnp.concatenate([tile] * 8, axis=0) * own
        real = rad[0, pl.ds(b * 8, 8)].reshape(256, 128)
        imag = rad[1, pl.ds(b * 8, 8)].reshape(256, 128)
        by_real = dot(spread, real)
        by_imag = dot(spread, imag)
        for i in range(8):
            lo = slice(i * 16, i * 16 + 8)
            hi = slice(i * 16 + 8, i * 16 + 16)
            leaf[pl.ds(i * 256 + b, 8, stride=32), :] = by_real[lo] - by_imag[hi]
            leaf[pl.ds((8 + i) * 256 + b, 8, stride=32), :] = by_imag[lo] + by_real[hi]
        return carry

    lax.fori_loop(0, BOXES, box, 0, unroll=2)


def pack_leaves(leaf, packed):
    left = lane_ids((256, 128)) < 64
    for c in range(2):
        for m in range(4):
            first = leaf[(c * 8 + 2 * m) * 256 : (c * 8 + 2 * m + 1) * 256, :]
            second = leaf[(c * 8 + 2 * m + 1) * 256 : (c * 8 + 2 * m + 2) * 256, :]
            lanes = slice((c * 4 + m) * 128, (c * 4 + m + 1) * 128)
            packed[0, :, lanes] = jnp.where(left, first, pltpu.roll(second, 64, 1)).astype(BF16)
            packed[1, :, lanes] = jnp.where(left, pltpu.roll(first, 64, 1), second).astype(BF16)


def spread_currents(window, part, ext):
    rows = lax.broadcasted_iota(jnp.int32, (128, 512), 0)
    columns = lane_ids((128, 512))
    copier = jnp.logical_and(rows // U == columns // 128, rows % U == columns % U)
    copier = copier.astype(F32).astype(BF16)

    def fill(g, carry):
        piece = window[part, :, pl.ds(pl.multiple_of(g * 2048, 2048), 2048)]
        stacked = jnp.concatenate([piece[:, k * 128 : k * 128 + 128] for k in range(16)], axis=0)
        wide = dot(stacked, copier).astype(BF16)
        for k in range(16):
            for j in range(4):
                row = part * NC + g * 64 + k * 4 + j
                ext[row] = wide[k * 16 : k * 16 + 16, j * 128 : j * 128 + 128]
        return carry

    lax.fori_loop(0, 4, fill, 0)


def near_box(b, blocks, where, ext, out):
    masks = [(lane_ids((16, 128)) // U == k).astype(F32).astype(BF16) for k in range(4)]
    own = lane_ids((16, 256)) // U
    gathered = []
    for i in range(8):
        halves = []
        for h in range(2):
            total = None
            for k in range(4):
                row = where[(h * 4 + k) * NC + b * 8 + i]
                piece = ext[row] * masks[k]
                total = piece if total is None else total + piece
            halves.append(total)
        gathered.append(jnp.concatenate(halves, axis=1))
    stacked = jnp.concatenate(gathered, axis=0)
    sums = []
    for c in range(2):
        result = dot_t(stacked, blocks[c, pl.ds(b * 8, 8)].reshape(256, 256))
        total = jnp.zeros((16, 256), F32)
        for i in range(8):
            total = jnp.where(own == i, result[i * 16 : i * 16 + 16], total)
        sums.append(total)
    real, imag = sums
    lanes = pl.ds(pl.multiple_of(b * 256, 256), 256)
    out[0:8, lanes] = real[0:8] - imag[8:16]
    out[8:16, lanes] = imag[0:8] + real[8:16]


def widen(rec, half, n, device, field):
    for k in range(4):
        value = rec[half, n, k // 2, k % 2].astype(F32)
        field[pl.ds(device * 256 + k, 32, stride=8), :] = value
        field[pl.ds(device * 256 + k + 4, 32, stride=8), :] = value


def translate_chunk(base, which_box, which_off, field, table, sums, out, chip):
    starts = [base + j * 4096 for j in range(IL)]
    for b in range(BOXES):
        total = None
        for j in range(IL):
            row = which_box[starts[j] + b]
            operator = which_off[starts[j] + b]
            term = field[pl.ds(row, 8), :] * table[pl.ds(operator, 8), :]
            total = term if total is None else total + term
        sums[b * 8 : b * 8 + 8, :] = total
    parts = [sums[pl.ds(k, BOXES, stride=8), :] for k in range(8)]
    out[chip, 0, 0] = (parts[0] - parts[5]).astype(BF16)
    out[chip, 0, 1] = (parts[1] + parts[4]).astype(BF16)
    out[chip, 1, 0] = (parts[2] - parts[7]).astype(BF16)
    out[chip, 1, 1] = (parts[3] + parts[6]).astype(BF16)


def unpack_fields(rec2, matrix, leaf):
    left = lane_ids((256, 128)) < 64
    for c in range(2):
        for half in range(2):
            rows = slice(c * 512 + half * 256, c * 512 + half * 256 + 256)
            results = []
            for p in range(2):
                pieces = []
                for block in range(8):
                    for c2 in range(2):
                        at = (p * 8 + block) * 4
                        pieces.append(rec2[at : at + 4, :, c2].reshape(256, 128))
                fields = jnp.concatenate(pieces, axis=1)
                results.append(dot_t(fields, matrix[rows, :]))
            for m in range(2):
                first = results[0][:, m * 128 : m * 128 + 128]
                second = results[1][:, m * 128 : m * 128 + 128]
                at = (c * 8 + half * 4 + m * 2) * 256
                leaf[at : at + 256, :] = jnp.where(left, first, pltpu.roll(second, 64, 1))
                leaf[at + 256 : at + 512, :] = jnp.where(left, pltpu.roll(first, 64, 1), second)


def far_boxes(leaf, rad, out):
    own = lane_ids((16, 256)) // U

    def box(b, carry):
        pieces = []
        for i in range(8):
            for c in range(2):
                pieces.append(leaf[pl.ds((c * 8 + i) * 256 + b, 8, stride=32), :])
        stacked = jnp.concatenate(pieces, axis=0).astype(BF16)
        sums = []
        for c in range(2):
            result = dot_t(stacked, rad[c, pl.ds(b * 8, 8)].reshape(256, 128))
            total = jnp.zeros((16, 256), F32)
            for i in range(8):
                total = jnp.where(own == i, result[i * 16 : i * 16 + 16], total)
            sums.append(total)
        real, imag = sums
        lanes = pl.ds(pl.multiple_of(b * 256, 256), 256)
        out[0:8, lanes] += real[0:8] + imag[8:16]
        out[8:16, lanes] += real[8:16] - imag[0:8]
        return carry

    lax.fori_loop(0, BOXES, box, 0, unroll=2)


def main_kernel(
    cur,
    blocks_in,
    rad_in,
    interp,
    angle,
    oper,
    list_in,
    count_in,
    box_in,
    off_in,
    out,
    matrix,
    trig,
    leaf,
    packed,
    rad,
    blocks,
    window,
    ext,
    send,
    rec,
    piece,
    pieces,
    field,
    table,
    sums,
    send2,
    rec2,
    rows_here,
    boxes_here,
    offs_here,
    where,
    which_box,
    which_off,
    load_sems,
    list_sems,
    box_sems,
    off_sems,
    up_send,
    up_recv,
    pass_send,
    pass_recv,
    down_send,
    down_recv,
    side_send,
    side_recv,
    own_sem,
):
    x, y, z, core = place()
    chip = x * 16 + y * 4 + z
    sibling = (x, (y * 4 + z) * 2 + 1 - core)
    device = chip * 2 + core
    other_at = lax.rem(device + 2 * core - 1 + 128, 128)
    other = (lax.div(other_at, 32), lax.rem(other_at, 32))

    def moved(n, sign):
        m = lax.rem((n + 1) * 37, CHIPS)
        step = (lax.div(m, 16), lax.rem(lax.div(m, 4), 4), lax.rem(m, 4))
        tx, ty, tz = [lax.rem(v + 4 + sign * s, 4) for v, s in zip((x, y, z), step)]
        return tx * 16 + ty * 4 + tz, (tx, (ty * 4 + tz) * 2 + core)

    loads = [
        pltpu.make_async_copy(cur, window.at[1], load_sems.at[0]),
        pltpu.make_async_copy(rad_in, rad, load_sems.at[1]),
        pltpu.make_async_copy(blocks_in, blocks, load_sems.at[2]),
    ]
    loads[0].start()
    loads[1].start()
    barrier = pltpu.get_barrier_semaphore()

    def greet(n, carry):
        pl.semaphore_signal(barrier, inc=1, device_id=moved(n, 1)[1], device_id_type=MESH_ID)
        return carry

    lax.fori_loop(0, CHIPS - 1, greet, 0)
    pl.semaphore_signal(barrier, inc=1, device_id=sibling, device_id_type=MESH_ID)
    pl.semaphore_signal(barrier, inc=1, device_id=other, device_id_type=MESH_ID)

    box_load = pltpu.make_async_copy(box_in, boxes_here, load_sems.at[4])
    off_load = pltpu.make_async_copy(off_in, offs_here, load_sems.at[5])
    slots = lax.broadcasted_iota(jnp.int32, (NBR, NC), 0)
    rows_here[...] = jnp.where(slots < count_in[...], list_in[...] - (device * NC - NC), 3 * NC)
    lists = []
    for k in range(NBR):
        lists.append(
            pltpu.make_async_copy(rows_here.at[k], where.at[pl.ds(k * NC, NC)], list_sems.at[k])
        )
        lists[-1].start()
    build_matrix(interp, angle, matrix, trig)
    piece[...] = jnp.zeros((32, 384), BF16)
    for c in range(2):
        piece[c * 16 : c * 16 + 16, 0:OFFS] = oper[c]
    loads[0].wait()
    loads[1].wait()
    loads[2].start()
    box_load.start()
    off_load.start()
    leaf_patterns(window.at[1], rad, leaf)
    pack_leaves(leaf, packed)
    for at in range(16):
        lanes = slice(at % 8 * 256, at % 8 * 256 + 256)
        result = dot(packed[at // 8], matrix[:, lanes]).astype(BF16)
        for r in range(R):
            for c in range(2):
                send[at * 4 + r // 2, r % 2, c] = result[r * 32 : r * 32 + 32, c * 128 : c * 128 + 128]

    pl.semaphore_wait(barrier, CHIPS + 1)

    def remote(src, dst, n, to):
        return pltpu.make_async_remote_copy(
            src_ref=src,
            dst_ref=dst,
            send_sem=side_send.at[n],
            recv_sem=side_recv.at[n],
            device_id=to,
            device_id_type=MESH_ID,
        )

    to_sibling = remote(window.at[1], window.at[2 * core], 0, sibling)
    to_other = remote(window.at[1], window.at[2 - 2 * core], 1, other)
    to_sibling.start()
    to_other.start()
    lines = []
    for s in range(3):
        tz = lax.rem(z + s + 1, 4)
        lines.append(remote(piece, pieces.at[z * 2 + core], 2 + s, (x, (y * 4 + tz) * 2 + core)))
        lines[-1].start()

    def up_copy(n):
        to, to_device = moved(n, 1)
        return pltpu.make_async_remote_copy(
            src_ref=send.at[to],
            dst_ref=rec.at[core, n],
            send_sem=up_send,
            recv_sem=up_recv.at[n],
            device_id=to_device,
            device_id_type=MESH_ID,
        )

    def up_start(n, carry):
        up_copy(n).start()
        return carry

    lax.fori_loop(0, WINDOW, up_start, 0)
    own_piece = pltpu.make_async_copy(piece, pieces.at[z * 2 + core], load_sems.at[3])
    own_piece.start()
    own = pltpu.make_async_copy(send.at[chip], rec.at[core, CHIPS - 1], own_sem)
    own.start()

    box_load.wait()
    off_load.wait()
    boxes_here[...] = boxes_here[...] * 8
    offs_here[...] = offs_here[...] * 8
    for j in range(IL):
        part = pl.ds(j * 4096, 4096)
        lists.append(pltpu.make_async_copy(boxes_here.at[j], which_box.at[part], box_sems.at[j]))
        lists[-1].start()
        lists.append(pltpu.make_async_copy(offs_here.at[j], which_off.at[part], off_sems.at[j]))
        lists[-1].start()

    own_piece.wait()
    for line in lines:
        line.wait()
    shares = []
    for s in range(4):
        at = pieces.at[s * 2 + core]
        shares.append(remote(at, at, 5 + s, sibling))
        shares[-1].start()
    own.wait()

    def pass_copy(m):
        at = rec.at[core, pl.ds(m * GROUP, GROUP)]
        return pltpu.make_async_remote_copy(
            src_ref=at,
            dst_ref=at,
            send_sem=pass_send,
            recv_sem=pass_recv.at[m],
            device_id=sibling,
            device_id_type=MESH_ID,
        )

    widen(rec, core, CHIPS - 1, 2 * chip + core, field)
    spread_currents(window, 1, ext)
    ext[3 * NC] = jnp.zeros((16, 128), BF16)
    to_sibling.wait()
    to_other.wait()
    spread_currents(window, 0, ext)
    spread_currents(window, 2, ext)
    for share in shares:
        share.wait()
    for c in range(2):
        rows = [pieces[m, c * 16 : c * 16 + 16, :] for m in range(8)]
        square = jnp.concatenate(rows, axis=0).astype(F32)
        for g in range(3):
            turned = square[:, g * 128 : g * 128 + 128].T
            for k in range(4):
                table[pl.ds(g * 1024 + c * 4 + k, 128, stride=8), :] = turned
    loads[2].wait()
    for copy in lists[:NBR]:
        copy.wait()

    def arrive(n):
        up_copy(n).wait_recv()

        @pl.when(n < CHIPS - 1 - WINDOW)
        def _():
            up_copy(n + WINDOW).start()

    def take(m):
        at = rec.at[1 - core, pl.ds(m * GROUP, GROUP)]
        pltpu.make_async_copy(at, at, pass_recv.at[m]).wait()
        for k in range(GROUP):
            n = m * GROUP + k
            widen(rec, 1 - core, n, 2 * moved(n, -1)[0] + 1 - core, field)

    def near_step(m, carry):
        near_box(2 * m, blocks, where, ext, out)
        near_box(2 * m + 1, blocks, where, ext, out)
        for k in range(GROUP - 1):
            arrive(m * GROUP + k)

        @pl.when(m < CHIPS // GROUP - 1)
        def _():
            arrive(m * GROUP + GROUP - 1)

        pass_copy(m).start()
        for k in range(GROUP - 1):
            n = m * GROUP + k
            widen(rec, core, n, 2 * moved(n, -1)[0] + core, field)

        @pl.when(m < CHIPS // GROUP - 1)
        def _():
            n = m * GROUP + GROUP - 1
            widen(rec, core, n, 2 * moved(n, -1)[0] + core, field)

        @pl.when(m >= 1)
        def _():
            take(m - 1)

        return carry

    lax.fori_loop(0, CHIPS // GROUP, near_step, 0)
    take(CHIPS // GROUP - 1)
    for copy in lists[NBR:]:
        copy.wait()

    def down_copy(n):
        to, to_device = moved(n, 1)
        return pltpu.make_async_remote_copy(
            src_ref=send2.at[to],
            dst_ref=rec2.at[chip],
            send_sem=down_send,
            recv_sem=down_recv,
            device_id=to_device,
            device_id_type=MESH_ID,
        )

    def chunk(n, carry):
        to = moved(n, 1)[0]
        base = to * 64 + core * 32
        translate_chunk(base, which_box, which_off, field, table, sums, send2, to)

        @pl.when(n < CHIPS - 1)
        def _():
            down_copy(n).start()

        return carry

    lax.fori_loop(0, CHIPS, chunk, 0)
    last = pltpu.make_async_copy(send2.at[chip], rec2.at[chip], own_sem)
    last.start()

    def settle(ref, sem):
        pltpu.make_async_copy(ref, ref, sem).wait()

    settle(send.at[pl.ds(0, CHIPS - 1)], up_send)
    settle(rec.at[core], pass_send)
    last.wait()

    settle(send2.at[pl.ds(0, CHIPS - 1)], down_send)
    settle(rec2.at[pl.ds(0, CHIPS - 1)], down_recv)
    unpack_fields(rec2, matrix, leaf)
    far_boxes(leaf, rad, out)


def main_part(cur, blocks, rad, interp, angle, oper, near_rows, near_count, box, off):
    any_spec = pl.BlockSpec(memory_space=pl.ANY)
    sems = pltpu.SemaphoreType.DMA
    return pl.pallas_call(
        main_kernel,
        out_shape=jax.ShapeDtypeStruct((16, NC * U), F32),
        in_specs=[any_spec] * 3 + [VMEM_SPEC] * 5 + [any_spec] * 2,
        out_specs=VMEM_SPEC,
        scratch_shapes=[
            pltpu.VMEM((1024, 2048), BF16),
            pltpu.VMEM((16, 1024), F32),
            pltpu.VMEM((16 * 256, 128), F32),
            pltpu.VMEM((2, 256, 1024), BF16),
            pltpu.VMEM((2, NC, U, 128), BF16),
            pltpu.VMEM((2, NC, U, NBR * U), BF16),
            pltpu.VMEM((3, 16, NC * U), BF16),
            pltpu.VMEM((3 * NC + 1, 16, 128), BF16),
            pltpu.VMEM((CHIPS, 2, 2, BOXES, 128), BF16),
            pltpu.VMEM((2, CHIPS, 2, 2, BOXES, 128), BF16),
            pltpu.VMEM((32, 384), BF16),
            pltpu.VMEM((8, 32, 384), BF16),
            pltpu.VMEM((4096 * 8, 128), F32),
            pltpu.VMEM((384 * 8, 128), F32),
            pltpu.VMEM((BOXES * 8, 128), F32),
            pltpu.VMEM((CHIPS, 2, 2, BOXES, 128), BF16),
            pltpu.VMEM((CHIPS, 2, 2, BOXES, 128), BF16),
            pltpu.VMEM((NBR, NC), jnp.int32),
            pltpu.VMEM((IL, 4096), jnp.int32),
            pltpu.VMEM((IL, 4096), jnp.int32),
            pltpu.SMEM((NC * NBR,), jnp.int32),
            pltpu.SMEM((4096 * IL,), jnp.int32),
            pltpu.SMEM((4096 * IL,), jnp.int32),
            sems((6,)),
            sems((NBR,)),
            sems((IL,)),
            sems((IL,)),
            sems,
            sems((CHIPS,)),
            sems,
            sems((CHIPS // GROUP,)),
            sems,
            sems,
            sems((9,)),
            sems((9,)),
            sems,
        ],
        compiler_params=pltpu.CompilerParams(
            collective_id=1, has_side_effects=True, vmem_limit_bytes=60 << 20
        ),
        name="up_near_translate",
    )(cur, blocks, rad, interp, angle, oper, near_rows, near_count, box, off)


def local(
    currents,
    near_blocks,
    near_list,
    near_count,
    radiation,
    interp,
    shift_angle,
    translation,
    trans_box,
    trans_off,
):
    out = main_part(
        currents.reshape(16, NC * U),
        near_blocks,
        radiation,
        interp,
        shift_angle,
        translation.transpose(0, 2, 1),
        near_list.T,
        near_count.reshape(1, NC),
        trans_box.T,
        trans_off.T,
    )
    return out.reshape(2, R, NC * U)


def solution(mesh):
    placed = (
        P(None, None, AXES),
        P(None, AXES, None, None),
        P(AXES, None),
        P(AXES),
        P(None, AXES, None, None),
        P(),
        P(),
        P(None, None, AXES),
        P(),
        P(),
    )
    return jax.shard_map(
        local, mesh=mesh, in_specs=placed, out_specs=P(None, None, AXES), check_vma=False
    )
```

```python
import jax
import jax.numpy as jnp
from jax import lax
from jax.experimental import pallas as pl
from jax.experimental.pallas import tpu as pltpu
from jax.sharding import PartitionSpec as P

R = 8
U = 32
NBR = 8
K0 = 64
K1 = 1024
IL = 12
NC = 256
OFFS = 316
BOXES = 32
WINDOW = 32
GROUP = 4
CHIPS = 64
AXES = ("grp", "smp")
MESH_ID = pl.DeviceIdType.MESH
F32 = jnp.float32
BF16 = jnp.bfloat16
VMEM_SPEC = pl.BlockSpec(memory_space=pltpu.VMEM)
SMEM_SPEC = pl.BlockSpec(memory_space=pltpu.SMEM)


def place():
    x = lax.axis_index("grp")
    smp = lax.axis_index("smp")
    core = lax.rem(smp, 2)
    y = lax.div(smp, 8)
    z = lax.rem(lax.div(smp, 2), 4)
    return x, y, z, core


def dot(left, right):
    return lax.dot_general(left, right, (((1,), (0,)), ((), ())), preferred_element_type=F32)


def dot_t(left, right):
    return lax.dot_general(left, right, (((1,), (1,)), ((), ())), preferred_element_type=F32)


def lane_ids(shape):
    return lax.broadcasted_iota(jnp.int32, shape, 1)


def build_matrix(interp, angle, matrix, trig):
    trig[0:8, :] = jnp.cos(angle[...])
    trig[8:16, :] = jnp.sin(angle[...])
    for block in range(8):
        lanes = slice(block * 128, block * 128 + 128)
        table = interp[:, lanes].astype(F32)
        for i in range(8):
            cosine = (table * trig[i : i + 1, lanes]).astype(BF16)
            sine_part = (table * trig[8 + i : 9 + i, lanes]).astype(BF16)
            first = slice(i * 64, i * 64 + 64)
            second = slice(512 + i * 64, 512 + i * 64 + 64)
            matrix[first, block * 256 : block * 256 + 128] = cosine
            matrix[first, block * 256 + 128 : block * 256 + 256] = sine_part
            matrix[second, block * 256 : block * 256 + 128] = -sine_part
            matrix[second, block * 256 + 128 : block * 256 + 256] = cosine


def leaf_patterns(cur, rad, leaf):
    own = lax.broadcasted_iota(jnp.int32, (128, 256), 0) // 16 == lane_ids((128, 256)) // U
    own = own.astype(F32).astype(BF16)

    def box(b, carry):
        tile = cur[:, pl.ds(pl.multiple_of(b * 256, 256), 256)]
        spread = jnp.concatenate([tile] * 8, axis=0) * own
        real = rad[0, pl.ds(b * 8, 8)].reshape(256, 128)
        imag = rad[1, pl.ds(b * 8, 8)].reshape(256, 128)
        by_real = dot(spread, real)
        by_imag = dot(spread, imag)
        for i in range(8):
            lo = slice(i * 16, i * 16 + 8)
            hi = slice(i * 16 + 8, i * 16 + 16)
            leaf[pl.ds(i * 256 + b, 8, stride=32), :] = by_real[lo] - by_imag[hi]
            leaf[pl.ds((8 + i) * 256 + b, 8, stride=32), :] = by_imag[lo] + by_real[hi]
        return carry

    lax.fori_loop(0, BOXES, box, 0, unroll=8)


def pack_leaves(leaf, packed):
    left = lane_ids((256, 128)) < 64
    for c in range(2):
        for m in range(4):
            first = leaf[(c * 8 + 2 * m) * 256 : (c * 8 + 2 * m + 1) * 256, :]
            second = leaf[(c * 8 + 2 * m + 1) * 256 : (c * 8 + 2 * m + 2) * 256, :]
            lanes = slice((c * 4 + m) * 128, (c * 4 + m + 1) * 128)
            packed[0, :, lanes] = jnp.where(left, first, pltpu.roll(second, 64, 1)).astype(BF16)
            packed[1, :, lanes] = jnp.where(left, pltpu.roll(first, 64, 1), second).astype(BF16)


def spread_currents(window, part, ext):
    rows = lax.broadcasted_iota(jnp.int32, (128, 512), 0)
    columns = lane_ids((128, 512))
    copier = jnp.logical_and(rows // U == columns // 128, rows % U == columns % U)
    copier = copier.astype(F32).astype(BF16)

    def fill(g, carry):
        piece = window[part, :, pl.ds(pl.multiple_of(g * 2048, 2048), 2048)]
        stacked = jnp.concatenate([piece[:, k * 128 : k * 128 + 128] for k in range(16)], axis=0)
        wide = dot(stacked, copier).astype(BF16)
        for k in range(16):
            for j in range(4):
                row = part * NC + g * 64 + k * 4 + j
                ext[row] = wide[k * 16 : k * 16 + 16, j * 128 : j * 128 + 128]
        return carry

    lax.fori_loop(0, 4, fill, 0)


def near_box(b, blocks, where, ext, out):
    masks = [(lane_ids((16, 128)) // U == k).astype(F32).astype(BF16) for k in range(4)]
    own = lane_ids((16, 256)) // U
    gathered = []
    for i in range(8):
        halves = []
        for h in range(2):
            total = None
            for k in range(4):
                row = where[(h * 4 + k) * NC + b * 8 + i]
                piece = ext[row] * masks[k]
                total = piece if total is None else total + piece
            halves.append(total)
        gathered.append(jnp.concatenate(halves, axis=1))
    stacked = jnp.concatenate(gathered, axis=0)
    sums = []
    for c in range(2):
        result = dot_t(stacked, blocks[c, pl.ds(b * 8, 8)].reshape(256, 256))
        total = jnp.zeros((16, 256), F32)
        for i in range(8):
            total = jnp.where(own == i, result[i * 16 : i * 16 + 16], total)
        sums.append(total)
    real, imag = sums
    lanes = pl.ds(pl.multiple_of(b * 256, 256), 256)
    out[0:8, lanes] = real[0:8] - imag[8:16]
    out[8:16, lanes] = imag[0:8] + real[8:16]


def widen(rec, half, n, device, field):
    for k in range(4):
        value = rec[half, n, k // 2, k % 2].astype(F32)
        field[pl.ds(device * 256 + k, 32, stride=8), :] = value
        field[pl.ds(device * 256 + k + 4, 32, stride=8), :] = value


def translate_chunk(base, which_box, which_off, field, table, sums):
    starts = [base + j * 4096 for j in range(IL)]
    for b in range(BOXES):
        total = None
        for j in range(IL):
            row = which_box[starts[j] + b]
            operator = which_off[starts[j] + b]
            term = field[pl.ds(row, 8), :] * table[pl.ds(operator, 8), :]
            total = term if total is None else total + term
        sums[b * 8 : b * 8 + 8, :] = total


def combine_chunk(sums, out, chip):
    parts = [sums[pl.ds(k, BOXES, stride=8), :] for k in range(8)]
    out[chip, 0, 0] = (parts[0] - parts[5]).astype(BF16)
    out[chip, 0, 1] = (parts[1] + parts[4]).astype(BF16)
    out[chip, 1, 0] = (parts[2] - parts[7]).astype(BF16)
    out[chip, 1, 1] = (parts[3] + parts[6]).astype(BF16)


def unpack_fields(rec2, matrix, leaf):
    left = lane_ids((256, 128)) < 64
    for c in range(2):
        for half in range(2):
            rows = slice(c * 512 + half * 256, c * 512 + half * 256 + 256)
            results = []
            for p in range(2):
                pieces = []
                for block in range(8):
                    for c2 in range(2):
                        at = (p * 8 + block) * 4
                        pieces.append(rec2[at : at + 4, :, c2].reshape(256, 128))
                fields = jnp.concatenate(pieces, axis=1)
                results.append(dot_t(fields, matrix[rows, :]))
            for m in range(2):
                first = results[0][:, m * 128 : m * 128 + 128]
                second = results[1][:, m * 128 : m * 128 + 128]
                at = (c * 8 + half * 4 + m * 2) * 256
                leaf[at : at + 256, :] = jnp.where(left, first, pltpu.roll(second, 64, 1))
                leaf[at + 256 : at + 512, :] = jnp.where(left, pltpu.roll(first, 64, 1), second)


def far_boxes(leaf, rad, out):
    own = lane_ids((16, 256)) // U

    def box(b, carry):
        pieces = []
        for i in range(8):
            for c in range(2):
                pieces.append(leaf[pl.ds((c * 8 + i) * 256 + b, 8, stride=32), :])
        stacked = jnp.concatenate(pieces, axis=0).astype(BF16)
        sums = []
        for c in range(2):
            result = dot_t(stacked, rad[c, pl.ds(b * 8, 8)].reshape(256, 128))
            total = jnp.zeros((16, 256), F32)
            for i in range(8):
                total = jnp.where(own == i, result[i * 16 : i * 16 + 16], total)
            sums.append(total)
        real, imag = sums
        lanes = pl.ds(pl.multiple_of(b * 256, 256), 256)
        out[0:8, lanes] += real[0:8] + imag[8:16]
        out[8:16, lanes] += real[8:16] - imag[0:8]
        return carry

    lax.fori_loop(0, BOXES, box, 0, unroll=8)


def main_kernel(
    cur,
    blocks_in,
    rad_in,
    interp,
    angle,
    oper,
    list_in,
    count_in,
    box_in,
    off_in,
    out,
    matrix,
    trig,
    leaf,
    packed,
    rad,
    blocks,
    window,
    ext,
    send,
    rec,
    piece,
    pieces,
    field,
    table,
    sums,
    send2,
    rec2,
    rows_here,
    boxes_here,
    offs_here,
    where,
    which_box,
    which_off,
    load_sems,
    list_sems,
    box_sems,
    off_sems,
    up_send,
    up_recv,
    pass_send,
    pass_recv,
    down_send,
    down_recv,
    side_send,
    side_recv,
    own_sem,
):
    x, y, z, core = place()
    chip = x * 16 + y * 4 + z
    sibling = (x, (y * 4 + z) * 2 + 1 - core)
    device = chip * 2 + core
    other_at = lax.rem(device + 2 * core - 1 + 128, 128)
    other = (lax.div(other_at, 32), lax.rem(other_at, 32))

    def moved(n, sign):
        m = lax.rem((n + 1) * 37, CHIPS)
        step = (lax.div(m, 16), lax.rem(lax.div(m, 4), 4), lax.rem(m, 4))
        tx, ty, tz = [lax.rem(v + 4 + sign * s, 4) for v, s in zip((x, y, z), step)]
        return tx * 16 + ty * 4 + tz, (tx, (ty * 4 + tz) * 2 + core)

    loads = [
        pltpu.make_async_copy(cur, window.at[1], load_sems.at[0]),
        pltpu.make_async_copy(rad_in, rad, load_sems.at[1]),
        pltpu.make_async_copy(blocks_in, blocks, load_sems.at[2]),
    ]
    loads[0].start()
    loads[1].start()
    barrier = pltpu.get_barrier_semaphore()

    def greet(n, carry):
        pl.semaphore_signal(barrier, inc=1, device_id=moved(n, 1)[1], device_id_type=MESH_ID)
        return carry

    lax.fori_loop(0, CHIPS - 1, greet, 0)
    pl.semaphore_signal(barrier, inc=1, device_id=sibling, device_id_type=MESH_ID)
    pl.semaphore_signal(barrier, inc=1, device_id=other, device_id_type=MESH_ID)

    box_load = pltpu.make_async_copy(box_in, boxes_here, load_sems.at[4])
    off_load = pltpu.make_async_copy(off_in, offs_here, load_sems.at[5])
    slots = lax.broadcasted_iota(jnp.int32, (NBR, NC), 0)
    rows_here[...] = jnp.where(slots < count_in[...], list_in[...] - (device * NC - NC), 3 * NC)
    lists = []
    for k in range(NBR):
        lists.append(
            pltpu.make_async_copy(rows_here.at[k], where.at[pl.ds(k * NC, NC)], list_sems.at[k])
        )
        lists[-1].start()
    build_matrix(interp, angle, matrix, trig)
    piece[...] = jnp.zeros((32, 384), BF16)
    for c in range(2):
        piece[c * 16 : c * 16 + 16, 0:OFFS] = oper[c]
    loads[0].wait()
    loads[1].wait()
    loads[2].start()
    box_load.start()
    off_load.start()
    leaf_patterns(window.at[1], rad, leaf)
    pack_leaves(leaf, packed)
    for at in range(16):
        lanes = slice(at % 8 * 256, at % 8 * 256 + 256)
        result = dot(packed[at // 8], matrix[:, lanes]).astype(BF16)
        for r in range(R):
            for c in range(2):
                send[at * 4 + r // 2, r % 2, c] = result[r * 32 : r * 32 + 32, c * 128 : c * 128 + 128]

    pl.semaphore_wait(barrier, CHIPS + 1)

    def remote(src, dst, n, to):
        return pltpu.make_async_remote_copy(
            src_ref=src,
            dst_ref=dst,
            send_sem=side_send.at[n],
            recv_sem=side_recv.at[n],
            device_id=to,
            device_id_type=MESH_ID,
        )

    to_sibling = remote(window.at[1], window.at[2 * core], 0, sibling)
    to_other = remote(window.at[1], window.at[2 - 2 * core], 1, other)
    to_sibling.start()
    to_other.start()
    lines = []
    for s in range(3):
        tz = lax.rem(z + s + 1, 4)
        lines.append(remote(piece, pieces.at[z * 2 + core], 2 + s, (x, (y * 4 + tz) * 2 + core)))
        lines[-1].start()

    def up_copy(n):
        to, to_device = moved(n, 1)
        return pltpu.make_async_remote_copy(
            src_ref=send.at[to],
            dst_ref=rec.at[core, n],
            send_sem=up_send,
            recv_sem=up_recv.at[n],
            device_id=to_device,
            device_id_type=MESH_ID,
        )

    def up_start(n, carry):
        up_copy(n).start()
        return carry

    lax.fori_loop(0, WINDOW, up_start, 0)
    own_piece = pltpu.make_async_copy(piece, pieces.at[z * 2 + core], load_sems.at[3])
    own_piece.start()
    own = pltpu.make_async_copy(send.at[chip], rec.at[core, CHIPS - 1], own_sem)
    own.start()

    box_load.wait()
    off_load.wait()
    boxes_here[...] = boxes_here[...] * 8
    offs_here[...] = offs_here[...] * 8
    for j in range(IL):
        part = pl.ds(j * 4096, 4096)
        lists.append(pltpu.make_async_copy(boxes_here.at[j], which_box.at[part], box_sems.at[j]))
        lists[-1].start()
        lists.append(pltpu.make_async_copy(offs_here.at[j], which_off.at[part], off_sems.at[j]))
        lists[-1].start()

    own_piece.wait()
    for line in lines:
        line.wait()
    shares = []
    for s in range(4):
        at = pieces.at[s * 2 + core]
        shares.append(remote(at, at, 5 + s, sibling))
        shares[-1].start()
    own.wait()

    def pass_copy(m):
        at = rec.at[core, pl.ds(m * GROUP, GROUP)]
        return pltpu.make_async_remote_copy(
            src_ref=at,
            dst_ref=at,
            send_sem=pass_send,
            recv_sem=pass_recv.at[m],
            device_id=sibling,
            device_id_type=MESH_ID,
        )

    widen(rec, core, CHIPS - 1, 2 * chip + core, field)
    spread_currents(window, 1, ext)
    ext[3 * NC] = jnp.zeros((16, 128), BF16)
    to_sibling.wait()
    to_other.wait()
    spread_currents(window, 0, ext)
    spread_currents(window, 2, ext)
    for share in shares:
        share.wait()
    for c in range(2):
        rows = [pieces[m, c * 16 : c * 16 + 16, :] for m in range(8)]
        square = jnp.concatenate(rows, axis=0).astype(F32)
        for g in range(3):
            turned = square[:, g * 128 : g * 128 + 128].T
            for k in range(4):
                table[pl.ds(g * 1024 + c * 4 + k, 128, stride=8), :] = turned
    loads[2].wait()
    for copy in lists[:NBR]:
        copy.wait()

    def arrive(n):
        up_copy(n).wait_recv()

        @pl.when(n < CHIPS - 1 - WINDOW)
        def _():
            up_copy(n + WINDOW).start()

    def take(m):
        at = rec.at[1 - core, pl.ds(m * GROUP, GROUP)]
        pltpu.make_async_copy(at, at, pass_recv.at[m]).wait()
        for k in range(GROUP):
            n = m * GROUP + k
            widen(rec, 1 - core, n, 2 * moved(n, -1)[0] + 1 - core, field)

    def near_step(m, carry):
        near_box(2 * m, blocks, where, ext, out)
        near_box(2 * m + 1, blocks, where, ext, out)
        for k in range(GROUP - 1):
            arrive(m * GROUP + k)

        @pl.when(m < CHIPS // GROUP - 1)
        def _():
            arrive(m * GROUP + GROUP - 1)

        pass_copy(m).start()
        for k in range(GROUP - 1):
            n = m * GROUP + k
            widen(rec, core, n, 2 * moved(n, -1)[0] + core, field)

        @pl.when(m < CHIPS // GROUP - 1)
        def _():
            n = m * GROUP + GROUP - 1
            widen(rec, core, n, 2 * moved(n, -1)[0] + core, field)

        @pl.when(m >= 1)
        def _():
            take(m - 1)

        return carry

    lax.fori_loop(0, CHIPS // GROUP, near_step, 0)
    take(CHIPS // GROUP - 1)
    for copy in lists[NBR:]:
        copy.wait()

    def down_copy(n):
        to, to_device = moved(n, 1)
        return pltpu.make_async_remote_copy(
            src_ref=send2.at[to],
            dst_ref=rec2.at[chip],
            send_sem=down_send,
            recv_sem=down_recv,
            device_id=to_device,
            device_id_type=MESH_ID,
        )

    def chunk(n, carry):
        combine_chunk(sums, send2, moved(n - 1, 1)[0])
        base = moved(n, 1)[0] * 64 + core * 32
        translate_chunk(base, which_box, which_off, field, table, sums)

        @pl.when(n >= 1)
        def _():
            down_copy(n - 1).start()

        return carry

    sums[...] = jnp.zeros((BOXES * 8, 128), F32)
    lax.fori_loop(0, CHIPS, chunk, 0)
    combine_chunk(sums, send2, chip)
    last = pltpu.make_async_copy(send2.at[chip], rec2.at[chip], own_sem)
    last.start()

    def settle(ref, sem):
        pltpu.make_async_copy(ref, ref, sem).wait()

    settle(send.at[pl.ds(0, CHIPS - 1)], up_send)
    settle(rec.at[core], pass_send)
    last.wait()

    settle(send2.at[pl.ds(0, CHIPS - 1)], down_send)
    settle(rec2.at[pl.ds(0, CHIPS - 1)], down_recv)
    unpack_fields(rec2, matrix, leaf)
    far_boxes(leaf, rad, out)


def main_part(cur, blocks, rad, interp, angle, oper, near_rows, near_count, box, off):
    any_spec = pl.BlockSpec(memory_space=pl.ANY)
    sems = pltpu.SemaphoreType.DMA
    return pl.pallas_call(
        main_kernel,
        out_shape=jax.ShapeDtypeStruct((16, NC * U), F32),
        in_specs=[any_spec] * 3 + [VMEM_SPEC] * 5 + [any_spec] * 2,
        out_specs=VMEM_SPEC,
        scratch_shapes=[
            pltpu.VMEM((1024, 2048), BF16),
            pltpu.VMEM((16, 1024), F32),
            pltpu.VMEM((16 * 256, 128), F32),
            pltpu.VMEM((2, 256, 1024), BF16),
            pltpu.VMEM((2, NC, U, 128), BF16),
            pltpu.VMEM((2, NC, U, NBR * U), BF16),
            pltpu.VMEM((3, 16, NC * U), BF16),
            pltpu.VMEM((3 * NC + 1, 16, 128), BF16),
            pltpu.VMEM((CHIPS, 2, 2, BOXES, 128), BF16),
            pltpu.VMEM((2, CHIPS, 2, 2, BOXES, 128), BF16),
            pltpu.VMEM((32, 384), BF16),
            pltpu.VMEM((8, 32, 384), BF16),
            pltpu.VMEM((4096 * 8, 128), F32),
            pltpu.VMEM((384 * 8, 128), F32),
            pltpu.VMEM((BOXES * 8, 128), F32),
            pltpu.VMEM((CHIPS, 2, 2, BOXES, 128), BF16),
            pltpu.VMEM((CHIPS, 2, 2, BOXES, 128), BF16),
            pltpu.VMEM((NBR, NC), jnp.int32),
            pltpu.VMEM((IL, 4096), jnp.int32),
            pltpu.VMEM((IL, 4096), jnp.int32),
            pltpu.SMEM((NC * NBR,), jnp.int32),
            pltpu.SMEM((4096 * IL,), jnp.int32),
            pltpu.SMEM((4096 * IL,), jnp.int32),
            sems((6,)),
            sems((NBR,)),
            sems((IL,)),
            sems((IL,)),
            sems,
            sems((CHIPS,)),
            sems,
            sems((CHIPS // GROUP,)),
            sems,
            sems,
            sems((9,)),
            sems((9,)),
            sems,
        ],
        compiler_params=pltpu.CompilerParams(
            collective_id=1, has_side_effects=True, vmem_limit_bytes=60 << 20
        ),
        name="up_near_translate",
    )(cur, blocks, rad, interp, angle, oper, near_rows, near_count, box, off)


def local(
    currents,
    near_blocks,
    near_list,
    near_count,
    radiation,
    interp,
    shift_angle,
    translation,
    trans_box,
    trans_off,
):
    out = main_part(
        currents.reshape(16, NC * U),
        near_blocks,
        radiation,
        interp,
        shift_angle,
        translation.transpose(0, 2, 1),
        near_list.T,
        near_count.reshape(1, NC),
        trans_box.T,
        trans_off.T,
    )
    return out.reshape(2, R, NC * U)


def solution(mesh):
    placed = (
        P(None, None, AXES),
        P(None, AXES, None, None),
        P(AXES, None),
        P(AXES),
        P(None, AXES, None, None),
        P(),
        P(),
        P(None, None, AXES),
        P(),
        P(),
    )
    return jax.shard_map(
        local, mesh=mesh, in_specs=placed, out_specs=P(None, None, AXES), check_vma=False
    )
```

```python
import jax
import jax.numpy as jnp
from jax import lax
from jax.experimental import pallas as pl
from jax.experimental.pallas import tpu as pltpu
from jax.sharding import PartitionSpec as P

R = 8
U = 32
NBR = 8
K0 = 64
K1 = 1024
IL = 12
NC = 256
OFFS = 316
BOXES = 32
WINDOW = 32
GROUP = 4
CHIPS = 64
AXES = ("grp", "smp")
MESH_ID = pl.DeviceIdType.MESH
F32 = jnp.float32
BF16 = jnp.bfloat16
VMEM_SPEC = pl.BlockSpec(memory_space=pltpu.VMEM)
SMEM_SPEC = pl.BlockSpec(memory_space=pltpu.SMEM)


def place():
    x = lax.axis_index("grp")
    smp = lax.axis_index("smp")
    core = lax.rem(smp, 2)
    y = lax.div(smp, 8)
    z = lax.rem(lax.div(smp, 2), 4)
    return x, y, z, core


def dot(left, right):
    return lax.dot_general(left, right, (((1,), (0,)), ((), ())), preferred_element_type=F32)


def dot_t(left, right):
    return lax.dot_general(left, right, (((1,), (1,)), ((), ())), preferred_element_type=F32)


def lane_ids(shape):
    return lax.broadcasted_iota(jnp.int32, shape, 1)


def build_matrix(interp, angle, matrix, trig):
    trig[0:8, :] = jnp.cos(angle[...])
    trig[8:16, :] = jnp.sin(angle[...])
    for block in range(8):
        lanes = slice(block * 128, block * 128 + 128)
        table = interp[:, lanes].astype(F32)
        for i in range(8):
            cosine = (table * trig[i : i + 1, lanes]).astype(BF16)
            sine_part = (table * trig[8 + i : 9 + i, lanes]).astype(BF16)
            first = slice(i * 64, i * 64 + 64)
            second = slice(512 + i * 64, 512 + i * 64 + 64)
            matrix[first, block * 256 : block * 256 + 128] = cosine
            matrix[first, block * 256 + 128 : block * 256 + 256] = sine_part
            matrix[second, block * 256 : block * 256 + 128] = -sine_part
            matrix[second, block * 256 + 128 : block * 256 + 256] = cosine


def leaf_patterns(cur, rad, leaf):
    own = lax.broadcasted_iota(jnp.int32, (128, 256), 0) // 16 == lane_ids((128, 256)) // U
    own = own.astype(F32).astype(BF16)

    def box(b, carry):
        tile = cur[:, pl.ds(pl.multiple_of(b * 256, 256), 256)]
        spread = jnp.concatenate([tile] * 8, axis=0) * own
        real = rad[0, pl.ds(b * 8, 8)].reshape(256, 128)
        imag = rad[1, pl.ds(b * 8, 8)].reshape(256, 128)
        by_real = dot(spread, real)
        by_imag = dot(spread, imag)
        for i in range(8):
            lo = slice(i * 16, i * 16 + 8)
            hi = slice(i * 16 + 8, i * 16 + 16)
            leaf[pl.ds(i * 256 + b, 8, stride=32), :] = by_real[lo] - by_imag[hi]
            leaf[pl.ds((8 + i) * 256 + b, 8, stride=32), :] = by_imag[lo] + by_real[hi]
        return carry

    lax.fori_loop(0, BOXES, box, 0, unroll=8)


def pack_leaves(leaf, packed):
    left = lane_ids((256, 128)) < 64
    for c in range(2):
        for m in range(4):
            first = leaf[(c * 8 + 2 * m) * 256 : (c * 8 + 2 * m + 1) * 256, :]
            second = leaf[(c * 8 + 2 * m + 1) * 256 : (c * 8 + 2 * m + 2) * 256, :]
            lanes = slice((c * 4 + m) * 128, (c * 4 + m + 1) * 128)
            packed[0, :, lanes] = jnp.where(left, first, pltpu.roll(second, 64, 1)).astype(BF16)
            packed[1, :, lanes] = jnp.where(left, pltpu.roll(first, 64, 1), second).astype(BF16)


def spread_currents(window, part, ext):
    rows = lax.broadcasted_iota(jnp.int32, (128, 512), 0)
    columns = lane_ids((128, 512))
    copier = jnp.logical_and(rows // U == columns // 128, rows % U == columns % U)
    copier = copier.astype(F32).astype(BF16)

    def fill(g, carry):
        piece = window[part, :, pl.ds(pl.multiple_of(g * 2048, 2048), 2048)]
        stacked = jnp.concatenate([piece[:, k * 128 : k * 128 + 128] for k in range(16)], axis=0)
        wide = dot(stacked, copier).astype(BF16)
        for k in range(16):
            for j in range(4):
                row = part * NC + g * 64 + k * 4 + j
                ext[row] = wide[k * 16 : k * 16 + 16, j * 128 : j * 128 + 128]
        return carry

    lax.fori_loop(0, 4, fill, 0)


def near_box(b, blocks, where, ext, out):
    masks = [(lane_ids((16, 128)) // U == k).astype(F32).astype(BF16) for k in range(4)]
    own = lane_ids((16, 256)) // U
    gathered = []
    for i in range(8):
        halves = []
        for h in range(2):
            total = None
            for k in range(4):
                row = where[(h * 4 + k) * NC + b * 8 + i]
                piece = ext[row] * masks[k]
                total = piece if total is None else total + piece
            halves.append(total)
        gathered.append(jnp.concatenate(halves, axis=1))
    stacked = jnp.concatenate(gathered, axis=0)
    sums = []
    for c in range(2):
        result = dot_t(stacked, blocks[c, pl.ds(b * 8, 8)].reshape(256, 256))
        total = jnp.zeros((16, 256), F32)
        for i in range(8):
            total = jnp.where(own == i, result[i * 16 : i * 16 + 16], total)
        sums.append(total)
    real, imag = sums
    lanes = pl.ds(pl.multiple_of(b * 256, 256), 256)
    out[0:8, lanes] = real[0:8] - imag[8:16]
    out[8:16, lanes] = imag[0:8] + real[8:16]


def widen(rec, half, n, device, field):
    for k in range(4):
        value = rec[half, n, k // 2, k % 2].astype(F32)
        field[pl.ds(device * 256 + k, 32, stride=8), :] = value
        field[pl.ds(device * 256 + k + 4, 32, stride=8), :] = value


def translate_chunk(base, which_box, which_off, field, table, sums):
    starts = [base + j * 4096 for j in range(IL)]
    for b in range(BOXES):
        total = None
        for j in range(IL):
            row = which_box[starts[j] + b]
            operator = which_off[starts[j] + b]
            term = field[pl.ds(row, 8), :] * table[pl.ds(operator, 8), :]
            total = term if total is None else total + term
        sums[b * 8 : b * 8 + 8, :] = total


def combine_chunk(sums, out, chip):
    parts = [sums[pl.ds(k, BOXES, stride=8), :] for k in range(8)]
    out[chip, 0, 0] = (parts[0] - parts[5]).astype(BF16)
    out[chip, 0, 1] = (parts[1] + parts[4]).astype(BF16)
    out[chip, 1, 0] = (parts[2] - parts[7]).astype(BF16)
    out[chip, 1, 1] = (parts[3] + parts[6]).astype(BF16)


def unpack_fields(rec2, matrix, leaf):
    left = lane_ids((256, 128)) < 64
    for c in range(2):
        for half in range(2):
            rows = slice(c * 512 + half * 256, c * 512 + half * 256 + 256)
            both = []
            for p in range(2):
                pieces = []
                for block in range(8):
                    for c2 in range(2):
                        at = (p * 8 + block) * 4
                        pieces.append(rec2[at : at + 4, :, c2].reshape(256, 128))
                both.append(jnp.concatenate(pieces, axis=1))
            result = dot_t(jnp.concatenate(both, axis=0), matrix[rows, :])
            results = [result[0:256], result[256:512]]
            for m in range(2):
                first = results[0][:, m * 128 : m * 128 + 128]
                second = results[1][:, m * 128 : m * 128 + 128]
                at = (c * 8 + half * 4 + m * 2) * 256
                leaf[at : at + 256, :] = jnp.where(left, first, pltpu.roll(second, 64, 1))
                leaf[at + 256 : at + 512, :] = jnp.where(left, pltpu.roll(first, 64, 1), second)


def far_boxes(leaf, rad, out):
    own = lane_ids((16, 256)) // U

    def box(b, carry):
        pieces = []
        for i in range(8):
            for c in range(2):
                pieces.append(leaf[pl.ds((c * 8 + i) * 256 + b, 8, stride=32), :])
        stacked = jnp.concatenate(pieces, axis=0).astype(BF16)
        sums = []
        for c in range(2):
            result = dot_t(stacked, rad[c, pl.ds(b * 8, 8)].reshape(256, 128))
            total = jnp.zeros((16, 256), F32)
            for i in range(8):
                total = jnp.where(own == i, result[i * 16 : i * 16 + 16], total)
            sums.append(total)
        real, imag = sums
        lanes = pl.ds(pl.multiple_of(b * 256, 256), 256)
        out[0:8, lanes] += real[0:8] + imag[8:16]
        out[8:16, lanes] += real[8:16] - imag[0:8]
        return carry

    lax.fori_loop(0, BOXES, box, 0, unroll=8)


def main_kernel(
    cur,
    blocks_in,
    rad_in,
    interp,
    angle,
    oper,
    list_in,
    count_in,
    box_in,
    off_in,
    out,
    matrix,
    trig,
    leaf,
    packed,
    rad,
    blocks,
    window,
    ext,
    send,
    rec,
    piece,
    pieces,
    field,
    table,
    sums,
    send2,
    rec2,
    rows_here,
    boxes_here,
    offs_here,
    where,
    which_box,
    which_off,
    load_sems,
    list_sems,
    box_sems,
    off_sems,
    up_send,
    up_recv,
    pass_send,
    pass_recv,
    down_send,
    down_recv,
    side_send,
    side_recv,
    own_sem,
):
    x, y, z, core = place()
    chip = x * 16 + y * 4 + z
    sibling = (x, (y * 4 + z) * 2 + 1 - core)
    device = chip * 2 + core
    other_at = lax.rem(device + 2 * core - 1 + 128, 128)
    other = (lax.div(other_at, 32), lax.rem(other_at, 32))

    def moved(n, sign):
        m = lax.rem((n + 1) * 37, CHIPS)
        step = (lax.div(m, 16), lax.rem(lax.div(m, 4), 4), lax.rem(m, 4))
        tx, ty, tz = [lax.rem(v + 4 + sign * s, 4) for v, s in zip((x, y, z), step)]
        return tx * 16 + ty * 4 + tz, (tx, (ty * 4 + tz) * 2 + core)

    loads = [
        pltpu.make_async_copy(cur, window.at[1], load_sems.at[0]),
        pltpu.make_async_copy(rad_in, rad, load_sems.at[1]),
        pltpu.make_async_copy(blocks_in, blocks, load_sems.at[2]),
    ]
    loads[0].start()
    loads[1].start()
    barrier = pltpu.get_barrier_semaphore()

    def greet(n, carry):
        pl.semaphore_signal(barrier, inc=1, device_id=moved(n, 1)[1], device_id_type=MESH_ID)
        return carry

    lax.fori_loop(0, CHIPS - 1, greet, 0)
    pl.semaphore_signal(barrier, inc=1, device_id=sibling, device_id_type=MESH_ID)
    pl.semaphore_signal(barrier, inc=1, device_id=other, device_id_type=MESH_ID)

    box_load = pltpu.make_async_copy(box_in, boxes_here, load_sems.at[4])
    off_load = pltpu.make_async_copy(off_in, offs_here, load_sems.at[5])
    slots = lax.broadcasted_iota(jnp.int32, (NBR, NC), 0)
    rows_here[...] = jnp.where(slots < count_in[...], list_in[...] - (device * NC - NC), 3 * NC)
    lists = []
    for k in range(NBR):
        lists.append(
            pltpu.make_async_copy(rows_here.at[k], where.at[pl.ds(k * NC, NC)], list_sems.at[k])
        )
        lists[-1].start()
    build_matrix(interp, angle, matrix, trig)
    piece[...] = jnp.zeros((32, 384), BF16)
    for c in range(2):
        piece[c * 16 : c * 16 + 16, 0:OFFS] = oper[c]
    loads[0].wait()
    loads[1].wait()
    loads[2].start()
    box_load.start()
    off_load.start()
    leaf_patterns(window.at[1], rad, leaf)
    pack_leaves(leaf, packed)
    for block in range(8):
        lanes = slice(block * 256, block * 256 + 256)
        result = dot(packed[...].reshape(512, 1024), matrix[:, lanes]).astype(BF16)
        for p in range(2):
            for r in range(R):
                rows = slice(p * 256 + r * 32, p * 256 + r * 32 + 32)
                for c in range(2):
                    at = (p * 8 + block) * 4 + r // 2
                    send[at, r % 2, c] = result[rows, c * 128 : c * 128 + 128]

    pl.semaphore_wait(barrier, CHIPS + 1)

    def remote(src, dst, n, to):
        return pltpu.make_async_remote_copy(
            src_ref=src,
            dst_ref=dst,
            send_sem=side_send.at[n],
            recv_sem=side_recv.at[n],
            device_id=to,
            device_id_type=MESH_ID,
        )

    to_sibling = remote(window.at[1], window.at[2 * core], 0, sibling)
    to_other = remote(window.at[1], window.at[2 - 2 * core], 1, other)
    to_sibling.start()
    to_other.start()
    lines = []
    for s in range(3):
        tz = lax.rem(z + s + 1, 4)
        lines.append(remote(piece, pieces.at[z * 2 + core], 2 + s, (x, (y * 4 + tz) * 2 + core)))
        lines[-1].start()

    def up_copy(n):
        to, to_device = moved(n, 1)
        return pltpu.make_async_remote_copy(
            src_ref=send.at[to],
            dst_ref=rec.at[core, n],
            send_sem=up_send,
            recv_sem=up_recv.at[n],
            device_id=to_device,
            device_id_type=MESH_ID,
        )

    def up_start(n, carry):
        up_copy(n).start()
        return carry

    lax.fori_loop(0, WINDOW, up_start, 0)
    own_piece = pltpu.make_async_copy(piece, pieces.at[z * 2 + core], load_sems.at[3])
    own_piece.start()
    own = pltpu.make_async_copy(send.at[chip], rec.at[core, CHIPS - 1], own_sem)
    own.start()

    box_load.wait()
    off_load.wait()
    boxes_here[...] = boxes_here[...] * 8
    offs_here[...] = offs_here[...] * 8
    for j in range(IL):
        part = pl.ds(j * 4096, 4096)
        lists.append(pltpu.make_async_copy(boxes_here.at[j], which_box.at[part], box_sems.at[j]))
        lists[-1].start()
        lists.append(pltpu.make_async_copy(offs_here.at[j], which_off.at[part], off_sems.at[j]))
        lists[-1].start()

    own_piece.wait()
    for line in lines:
        line.wait()
    shares = []
    for s in range(4):
        at = pieces.at[s * 2 + core]
        shares.append(remote(at, at, 5 + s, sibling))
        shares[-1].start()
    own.wait()

    def pass_copy(m):
        at = rec.at[core, pl.ds(m * GROUP, GROUP)]
        return pltpu.make_async_remote_copy(
            src_ref=at,
            dst_ref=at,
            send_sem=pass_send,
            recv_sem=pass_recv.at[m],
            device_id=sibling,
            device_id_type=MESH_ID,
        )

    widen(rec, core, CHIPS - 1, 2 * chip + core, field)
    spread_currents(window, 1, ext)
    ext[3 * NC] = jnp.zeros((16, 128), BF16)
    to_sibling.wait()
    to_other.wait()
    spread_currents(window, 0, ext)
    spread_currents(window, 2, ext)
    for share in shares:
        share.wait()
    for c in range(2):
        rows = [pieces[m, c * 16 : c * 16 + 16, :] for m in range(8)]
        square = jnp.concatenate(rows, axis=0).astype(F32)
        for g in range(3):
            turned = square[:, g * 128 : g * 128 + 128].T
            for k in range(4):
                table[pl.ds(g * 1024 + c * 4 + k, 128, stride=8), :] = turned
    loads[2].wait()
    for copy in lists[:NBR]:
        copy.wait()

    def arrive(n):
        up_copy(n).wait_recv()

        @pl.when(n < CHIPS - 1 - WINDOW)
        def _():
            up_copy(n + WINDOW).start()

    def take(m):
        at = rec.at[1 - core, pl.ds(m * GROUP, GROUP)]
        pltpu.make_async_copy(at, at, pass_recv.at[m]).wait()
        for k in range(GROUP):
            n = m * GROUP + k
            widen(rec, 1 - core, n, 2 * moved(n, -1)[0] + 1 - core, field)

    def near_step(m, carry):
        near_box(2 * m, blocks, where, ext, out)
        near_box(2 * m + 1, blocks, where, ext, out)
        for k in range(GROUP - 1):
            arrive(m * GROUP + k)

        @pl.when(m < CHIPS // GROUP - 1)
        def _():
            arrive(m * GROUP + GROUP - 1)

        pass_copy(m).start()
        for k in range(GROUP - 1):
            n = m * GROUP + k
            widen(rec, core, n, 2 * moved(n, -1)[0] + core, field)

        @pl.when(m < CHIPS // GROUP - 1)
        def _():
            n = m * GROUP + GROUP - 1
            widen(rec, core, n, 2 * moved(n, -1)[0] + core, field)

        @pl.when(m >= 1)
        def _():
            take(m - 1)

        return carry

    lax.fori_loop(0, CHIPS // GROUP, near_step, 0)
    take(CHIPS // GROUP - 1)
    for copy in lists[NBR:]:
        copy.wait()

    def down_copy(n):
        to, to_device = moved(n, 1)
        return pltpu.make_async_remote_copy(
            src_ref=send2.at[to],
            dst_ref=rec2.at[chip],
            send_sem=down_send,
            recv_sem=down_recv,
            device_id=to_device,
            device_id_type=MESH_ID,
        )

    def chunk(n, carry):
        combine_chunk(sums, send2, moved(n - 1, 1)[0])
        base = moved(n, 1)[0] * 64 + core * 32
        translate_chunk(base, which_box, which_off, field, table, sums)

        @pl.when(n >= 1)
        def _():
            down_copy(n - 1).start()

        return carry

    sums[...] = jnp.zeros((BOXES * 8, 128), F32)
    lax.fori_loop(0, CHIPS, chunk, 0)
    combine_chunk(sums, send2, chip)
    last = pltpu.make_async_copy(send2.at[chip], rec2.at[chip], own_sem)
    last.start()

    def settle(ref, sem):
        pltpu.make_async_copy(ref, ref, sem).wait()

    settle(send.at[pl.ds(0, CHIPS - 1)], up_send)
    settle(rec.at[core], pass_send)
    last.wait()

    settle(send2.at[pl.ds(0, CHIPS - 1)], down_send)
    settle(rec2.at[pl.ds(0, CHIPS - 1)], down_recv)
    unpack_fields(rec2, matrix, leaf)
    far_boxes(leaf, rad, out)


def main_part(cur, blocks, rad, interp, angle, oper, near_rows, near_count, box, off):
    any_spec = pl.BlockSpec(memory_space=pl.ANY)
    sems = pltpu.SemaphoreType.DMA
    return pl.pallas_call(
        main_kernel,
        out_shape=jax.ShapeDtypeStruct((16, NC * U), F32),
        in_specs=[any_spec] * 3 + [VMEM_SPEC] * 5 + [any_spec] * 2,
        out_specs=VMEM_SPEC,
        scratch_shapes=[
            pltpu.VMEM((1024, 2048), BF16),
            pltpu.VMEM((16, 1024), F32),
            pltpu.VMEM((16 * 256, 128), F32),
            pltpu.VMEM((2, 256, 1024), BF16),
            pltpu.VMEM((2, NC, U, 128), BF16),
            pltpu.VMEM((2, NC, U, NBR * U), BF16),
            pltpu.VMEM((3, 16, NC * U), BF16),
            pltpu.VMEM((3 * NC + 1, 16, 128), BF16),
            pltpu.VMEM((CHIPS, 2, 2, BOXES, 128), BF16),
            pltpu.VMEM((2, CHIPS, 2, 2, BOXES, 128), BF16),
            pltpu.VMEM((32, 384), BF16),
            pltpu.VMEM((8, 32, 384), BF16),
            pltpu.VMEM((4096 * 8, 128), F32),
            pltpu.VMEM((384 * 8, 128), F32),
            pltpu.VMEM((BOXES * 8, 128), F32),
            pltpu.VMEM((CHIPS, 2, 2, BOXES, 128), BF16),
            pltpu.VMEM((CHIPS, 2, 2, BOXES, 128), BF16),
            pltpu.VMEM((NBR, NC), jnp.int32),
            pltpu.VMEM((IL, 4096), jnp.int32),
            pltpu.VMEM((IL, 4096), jnp.int32),
            pltpu.SMEM((NC * NBR,), jnp.int32),
            pltpu.SMEM((4096 * IL,), jnp.int32),
            pltpu.SMEM((4096 * IL,), jnp.int32),
            sems((6,)),
            sems((NBR,)),
            sems((IL,)),
            sems((IL,)),
            sems,
            sems((CHIPS,)),
            sems,
            sems((CHIPS // GROUP,)),
            sems,
            sems,
            sems((9,)),
            sems((9,)),
            sems,
        ],
        compiler_params=pltpu.CompilerParams(
            collective_id=1, has_side_effects=True, vmem_limit_bytes=60 << 20
        ),
        name="up_near_translate",
    )(cur, blocks, rad, interp, angle, oper, near_rows, near_count, box, off)


def local(
    currents,
    near_blocks,
    near_list,
    near_count,
    radiation,
    interp,
    shift_angle,
    translation,
    trans_box,
    trans_off,
):
    out = main_part(
        currents.reshape(16, NC * U),
        near_blocks,
        radiation,
        interp,
        shift_angle,
        translation.transpose(0, 2, 1),
        near_list.T,
        near_count.reshape(1, NC),
        trans_box.T,
        trans_off.T,
    )
    return out.reshape(2, R, NC * U)


def solution(mesh):
    placed = (
        P(None, None, AXES),
        P(None, AXES, None, None),
        P(AXES, None),
        P(AXES),
        P(None, AXES, None, None),
        P(),
        P(),
        P(None, None, AXES),
        P(),
        P(),
    )
    return jax.shard_map(
        local, mesh=mesh, in_specs=placed, out_specs=P(None, None, AXES), check_vma=False
    )
```
